32 devices in a mesh: row: 4 (over z), col: 8 (over y, x, core).
Axes of the slice: x: 2, y: 2, z: 4, core: 2. Of those that a mesh axis runs over, the one named last changes fastest.
Arguments:
- tokens: bfloat16 [10240, 2048], P('row', 'col'), may hold values from -6 to 6
- attn_norm: float32 [2048], replicated, may hold values from 0.5 to 1.5
- w_query: bfloat16 [2048, 2048], P('row', 'col'), may hold values from -0.125 to 0.125
- w_key: bfloat16 [2048, 2048], P('row', 'col'), may hold values from -0.125 to 0.125
- w_value: bfloat16 [2048, 2048], P('row', 'col'), may hold values from -0.125 to 0.125
- q_norm: float32 [2048], replicated, may hold values from 0.5 to 1.5
- k_norm: float32 [2048], replicated, may hold values from 0.5 to 1.5
- w_out: bfloat16 [2048, 2048], P('row', 'col'), may hold values from -1 to 1
- moe_norm: float32 [2048], replicated, may hold values from 0.5 to 1.5
- w_gate: bfloat16 [2048, 65536], P('row', 'col'), may hold values from -0.125 to 0.125
- w_up: bfloat16 [2048, 65536], P('row', 'col'), may hold values from -0.125 to 0.125
- w_down: bfloat16 [2048, 65536], P('row', 'col'), may hold values from -0.1875 to 0.1875
- routes: int32 [10240, 8], P('row'), may hold values from 0 to 63, all different within a row; in each aligned block of 2560 rows (0 to 2559, 2560 to 5119, ...) at most 426 rows name the same one
- gates: float32 [10240, 8], P('row'), may hold values from 0.2 to 0.6
- parents: int32 [4, 20], P('row'), may hold values from -1 to 7, as said below
- cotangent: bfloat16 [10240, 2048], P('row', 'col'), may hold values from -6 to 6
Outputs:
- output: bfloat16 [10240, 2048], P('row', 'col')
- tokens_grad: float32 [10240, 2048], P('row', 'col')
- attn_norm_grad: float32 [2048], P('col')
- w_query_grad: float32 [2048, 2048], P('row', 'col')
- w_key_grad: float32 [2048, 2048], P('row', 'col')
- w_value_grad: float32 [2048, 2048], P('row', 'col')
- q_norm_grad: float32 [2048], P('col')
- k_norm_grad: float32 [2048], P('col')
- w_out_grad: float32 [2048, 2048], P('row', 'col')
- moe_norm_grad: float32 [2048], P('col')
- w_gate_grad: float32 [2048, 65536], P('row', 'col')
- w_up_grad: float32 [2048, 65536], P('row', 'col')
- w_down_grad: float32 [2048, 65536], P('row', 'col')
The draws below stay inside these ranges and needn't reach their ends.
Inputs may be any that keep to these rules, and one draw needn't show every extreme that they name: `routes`: each row names 8 different experts; within each aligned block of 2560 rows no expert is named by more than 426 rows, a bound that some block reaches. `parents`: in every tree, segments 0 to 3 form a chain (segment 0 has parent -1, each next one the one before); the next 4 segments have the trunk's last segment as parent; the next 8 segments each have one of those branch segments as parent, 2 leaves to every branch; the last 4 segments have parent -1.
All inputs are finite; a program needn't handle non-finite values.
Results may differ from the reference program's by a relative error of at most 0.018.
Values may be sent and summed in bfloat16 or wider, within the bound.
No kernel may reach another device: no remote copies, remote signals or barrier semaphores. Data moves between devices by JAX's collectives and lax.ppermute only.
A program may use at most 512 MiB of HBM per device.

```python
import math
import jax
import jax.numpy as jnp
import numpy as np
from jax import lax

D = 2048
HEADS = 16
HD = 128
EXPERTS = 64
FF = 1024
TOPK = 8
SEG = 128
TRUNK = 512
BRANCHES = 4
LEAVES = 2
PADSEG = 4
TREES = 1
TREE = 2560
NSEG = 20
TOK_ROW = 2560
TOKENS = 10240
NTREES = 4
CAP = 426
QB = 512


def draw_parents(key, part):
    key = jax.random.fold_in(key, 7)
    trunk_count = TRUNK // SEG
    chain = jnp.arange(trunk_count, dtype=jnp.int32) - 1
    branch_parent = jnp.full((BRANCHES,), trunk_count - 1, jnp.int32)
    padding = jnp.full((PADSEG,), -1, jnp.int32)
    tree_keys = jax.random.split(key, NTREES)

    def one_tree(tree_key):
        order = jax.random.permutation(tree_key, BRANCHES * LEAVES).astype(jnp.int32)
        leaf_parent = (trunk_count + order // LEAVES).astype(jnp.int32)
        return jnp.concatenate([chain, branch_parent, leaf_parent, padding]).astype(jnp.int32)
    return jax.vmap(one_tree)(tree_keys)


def levels(rng, dims, cuts, low, largest):
    loudness, own = 1.0, jax.random.fold_in(rng, 6)
    for dim, shards_of in cuts:
        heights = jnp.exp(jax.random.uniform(jax.random.fold_in(own, dim), (shards_of,), jnp.float32, low / len(cuts), largest / len(cuts)))
        loudness = loudness * jnp.repeat(heights, dims[dim] // shards_of).reshape([-1 if axis == dim else 1 for axis in range(len(dims))])
    return loudness


def shared_out(stream_key, own, number, rows, number_of, top, bound, slope):
    ranking = jax.random.permutation(stream_key, number_of)
    packed, common = shares(number_of, rows * top, bound, slope, True), shares(number_of, rows * top, bound, slope, False)
    places = jnp.arange(number_of)

    def named(tallies, turn):
        used = int((tallies > 0).sum())
        fixed = max(1, used // 4)
        moved = fixed + (places - fixed + turn * (used - fixed)) % max(1, number_of - fixed)
        return jnp.zeros((number_of,), jnp.int32).at[ranking[jnp.where(places < fixed, places, moved)]].set(jnp.asarray(tallies, jnp.int32))

    tallies = jnp.where(number % 4 == 0, named(packed, number // 4), named(common, number - number // 4 - 1))
    mixed = jax.random.permutation(jax.random.fold_in(own, 3), number_of)
    giver, sink = mixed[0:number_of // 2 * 2:2], mixed[1:number_of // 2 * 2:2]
    slack = jnp.minimum(tallies[giver] - 1, bound - tallies[sink]) // 2
    slack = jnp.where((giver == ranking[0]) | (sink == ranking[0]) | (tallies[sink] == 0), 0, jnp.maximum(slack, 0))
    moved = jax.random.randint(jax.random.fold_in(own, 4), (number_of // 2,), 0, 1 << 20) % (slack + 1)
    tallies = tallies.at[giver].add(-moved).at[sink].add(moved)
    members = jnp.searchsorted(jnp.cumsum(tallies), jnp.arange(rows * top), side="right").astype(jnp.int32)
    table = members.reshape(top, rows).T
    table = table[jax.random.permutation(jax.random.fold_in(own, 1), rows)]
    turn = jax.random.randint(jax.random.fold_in(own, 2), (rows, 1), 0, top)
    return jnp.take_along_axis(table, (jnp.arange(top)[None, :] + turn) % top, axis=1)


def shares(amount, total, bound, lean, full):
    portions = [(1 << 20) // math.isqrt(standing ** lean) + 1 for standing in range(1, amount + 1)]
    largest = bound if full else min(bound, max(-(-total // amount), total * portions[0] // sum(portions)))
    least = 1 if total - largest >= amount - 1 else 0
    counts, rest = [largest] + [least] * (amount - 1), total - largest - least * (amount - 1)
    while rest > 0:
        free = [i for i in range(1, amount) if counts[i] < largest] or [i for i in range(1, amount) if counts[i] < bound]
        whole, budget = sum([portions[i] for i in free]), rest
        for i in free:
            addition = min(bound - counts[i], max(1, budget * portions[i] // whole), rest)
            counts[i] = counts[i] + addition
            rest = rest - addition
    return np.array(counts)


def gaussian(rng, dims, deviation, limit, cuts=(), held_as=jnp.bfloat16):
    values = jax.random.normal(rng, dims, jnp.float32) * deviation
    if len(cuts) > 0:
        values = levels(rng, dims, cuts, -0.22, 0.18) * values
    return jnp.clip(values, min=-limit, max=limit).astype(held_as)


def setup_inputs(seed: int = 0) -> dict:
    splits = jax.random.split(jax.random.key(seed), 17)
    tokens = gaussian(splits[0], (TOKENS, D), 1.0, 6.0, ((0, 4), (1, 8)))
    attn_norm = jnp.clip(1.0 + 0.1 * jax.random.normal(splits[1], (D,), jnp.float32), 0.5, 1.5)
    w_query = gaussian(splits[2], (D, D), D ** -0.5, 0.125, ((0, 4), (1, 8)))
    w_key = gaussian(splits[3], (D, D), D ** -0.5, 0.125, ((0, 4), (1, 8)))
    w_value = gaussian(splits[4], (D, D), D ** -0.5, 0.125, ((0, 4), (1, 8)))
    q_norm = jnp.clip(1.0 + 0.1 * jax.random.normal(splits[5], (D,), jnp.float32), 0.5, 1.5)
    k_norm = jnp.clip(1.0 + 0.1 * jax.random.normal(splits[6], (D,), jnp.float32), 0.5, 1.5)
    w_out = gaussian(splits[7], (D, D), (D // 64) ** -0.5, 1.0, ((0, 4), (1, 8)))
    moe_norm = jnp.clip(1.0 + 0.1 * jax.random.normal(splits[8], (D,), jnp.float32), 0.5, 1.5)
    w_gate = gaussian(splits[9], (D, EXPERTS * FF), D ** -0.5, 0.125, ((0, 4), (1, 8)))
    w_up = gaussian(splits[10], (D, EXPERTS * FF), D ** -0.5, 0.125, ((0, 4), (1, 8)))
    w_down = gaussian(splits[11], (D, EXPERTS * FF), FF ** -0.5, 0.1875, ((0, 4), (1, 8)))
    routes_keys = jax.random.split(jax.random.fold_in(splits[12], 1), TOKENS // TOK_ROW)
    routes_turns = jax.random.permutation(jax.random.fold_in(splits[12], 3), TOKENS // TOK_ROW)
    routes = jax.vmap(lambda own, number: shared_out(jax.random.fold_in(splits[12], 2), own, number, TOK_ROW, EXPERTS, TOPK, CAP, 1))(routes_keys, routes_turns).reshape((TOKENS, TOPK))
    gates = jnp.clip(0.2 + 0.400000021 * jax.random.uniform(splits[13], (TOKENS, TOPK), jnp.float32) ** levels(splits[13], (TOKENS, TOPK), ((0, 4),), -0.2, 0.2), 0.2, 0.6)
    parents = draw_parents(jax.random.fold_in(splits[16], 71), 0)
    cotangent = gaussian(splits[15], (TOKENS, D), 1.0, 6.0, ((0, 4), (1, 8)))
    return {"tokens": tokens, "attn_norm": attn_norm, "w_query": w_query, "w_key": w_key, "w_value": w_value, "q_norm": q_norm, "k_norm": k_norm, "w_out": w_out, "moe_norm": moe_norm, "w_gate": w_gate, "w_up": w_up, "w_down": w_down, "routes": routes, "gates": gates, "parents": parents, "cotangent": cotangent}


EPS = 1e-05
NEGATIVE = -1e+30
HIGHEST = lax.Precision.HIGHEST

@jax.custom_vjp
def low(v):
    return lax.optimization_barrier(v.astype(jnp.bfloat16)).astype(jnp.float32)

@jax.custom_vjp
def low_back(v):
    return v

def low_keep(v):
    return (low(v), None)

def low_pass(kept, grad):
    return (grad,)

def back_keep(v):
    return (v, None)

def back_low(kept, grad):
    return (low(grad),)
low.defvjp(low_keep, low_pass)
low_back.defvjp(back_keep, back_low)

def ancestry(parent_ids):
    segment_ids = jnp.arange(NSEG, dtype=jnp.int32)

    def advance(turn_index, loop_state):
        current, reached = loop_state
        matches = current[:, None] == segment_ids[None, :]
        reached = reached + matches.astype(jnp.int32)
        parent_of = lax.optimization_barrier(jnp.sum(jnp.where(matches, parent_ids[None, :], 0), 1)).astype(jnp.int32)
        current = jnp.where(current >= 0, parent_of, -1).astype(jnp.int32)
        return (current, reached)
    start_state = (segment_ids, jnp.zeros((NSEG, NSEG), jnp.int32))
    return lax.fori_loop(0, NSEG, advance, start_state)[1]

def block_mask(ancestors, begin):
    segment_ids = jnp.arange(NSEG, dtype=jnp.int32)
    query_pos = begin + jnp.arange(QB, dtype=jnp.int32)
    key_pos = jnp.arange(TREE, dtype=jnp.int32)
    picks = (query_pos[:, None] // SEG == segment_ids[None, :]).astype(jnp.float32)
    visible = jnp.dot(picks, ancestors.astype(jnp.float32))
    visible = jnp.repeat(visible, SEG, axis=1) > 0.5
    same_seg = query_pos[:, None] // SEG == key_pos[None, :] // SEG
    return visible & (jnp.logical_not(same_seg) | (key_pos[None, :] <= query_pos[:, None]))

def rope_tables(ancestors):
    depths = (lax.optimization_barrier(jnp.sum(ancestors, 1)) - 1).astype(jnp.int32)
    position = jnp.arange(TREE, dtype=jnp.int32)
    places = (jnp.repeat(depths, SEG) * SEG + position % SEG).astype(jnp.float32)
    frequency = jnp.exp(jnp.arange(HD // 2, dtype=jnp.float32) * (-2.0 * math.log(10000.0) / HD))
    angles = places[:, None] * frequency[None, :]
    return (jnp.cos(angles), jnp.sin(angles))

def rotate(field, cos_table, sin_table):
    half_width = field.shape[-1] // 2
    first_half = field[..., :half_width]
    second_half = field[..., half_width:]
    cosine = cos_table[:, None, :]
    sine_part = sin_table[:, None, :]
    return jnp.concatenate([first_half * cosine - second_half * sine_part, second_half * cosine + first_half * sine_part], -1)

def dispatch(route_rows, gate_rows, first_expert, expert_count):
    pair_count = route_rows.shape[0] * route_rows.shape[1]
    local_ids = route_rows.reshape(-1) - first_expert
    expert_ids = jnp.arange(expert_count, dtype=jnp.int32)
    onehot = (local_ids[:, None] == expert_ids[None, :]).astype(jnp.int32)
    rank_in = (jnp.cumsum(onehot, 0) - 1).astype(jnp.int32)
    slot_index = lax.optimization_barrier(jnp.sum(onehot * (rank_in + expert_ids[None, :] * CAP), 1)).astype(jnp.int32)
    is_local = lax.optimization_barrier(jnp.sum(onehot, 1)) > 0
    slot_index = jnp.where(is_local, slot_index, expert_count * CAP).astype(jnp.int32)
    token_index = (jnp.arange(pair_count, dtype=jnp.int32) // route_rows.shape[1]).astype(jnp.int32)
    slot_token = jnp.full((expert_count * CAP + 1,), route_rows.shape[0], jnp.int32).at[slot_index].set(token_index)[:expert_count * CAP]
    slot_gate = jnp.zeros((expert_count * CAP + 1,), jnp.float32).at[slot_index].set(gate_rows.reshape(-1))[:expert_count * CAP]
    return (slot_token, slot_gate)

def dispatch_all(route_rows, gate_rows):
    return dispatch(route_rows, gate_rows, 0, EXPERTS)

def attend_tree(parts):
    query_t, key_t, value_t, ancestors = parts
    scale_factor = 1.0 / math.sqrt(HD)

    def one_block(begin):
        query_block = lax.dynamic_slice_in_dim(query_t, begin, QB, 0)
        scores = low_back(jnp.einsum('qhd,khd->hqk', query_block, key_t, precision=HIGHEST) * scale_factor)
        allowed = block_mask(ancestors, begin)
        scores = jnp.where(allowed[None], scores, NEGATIVE)
        highest = lax.optimization_barrier(jnp.max(scores, -1, keepdims=True))
        raised = jnp.exp(scores - highest)
        weights = low(raised / lax.optimization_barrier(jnp.sum(raised, -1, keepdims=True)))
        return jnp.einsum('hqk,khd->qhd', weights, value_t, precision=HIGHEST)
    blocks = lax.map(jax.checkpoint(one_block), jnp.arange(TREE // QB, dtype=jnp.int32) * QB)
    return blocks.reshape(TREE, HEADS, HD)

def group_experts(normed, slot_token, slot_gate, gate_w, up_w, down_w):
    padded = jnp.concatenate([normed, jnp.zeros((1, D), jnp.float32)], 0)
    expert_in = padded[slot_token].reshape(EXPERTS, CAP, D)
    gate_act = low_back(jnp.einsum('ecd,def->ecf', expert_in, gate_w.reshape(D, EXPERTS, FF), precision=HIGHEST))
    up_act = low_back(jnp.einsum('ecd,def->ecf', expert_in, up_w.reshape(D, EXPERTS, FF), precision=HIGHEST))
    hidden = low(jax.nn.silu(gate_act) * up_act)
    expert_out = low_back(jnp.einsum('ecf,def->ecd', hidden, down_w.reshape(D, EXPERTS, FF), precision=HIGHEST))
    summed = jnp.zeros((TOK_ROW + 1, D), jnp.float32).at[slot_token].add(slot_gate[:, None] * expert_out.reshape(-1, D))
    return summed[:TOK_ROW]

def reference(tokens, attn_norm, w_query, w_key, w_value, q_norm, k_norm, w_out, moe_norm, w_gate, w_up, w_down, routes, gates, parents, cotangent):
    groups = NTREES // TREES
    ancestors = jax.vmap(ancestry)(parents)
    cos_table, sin_table = jax.vmap(rope_tables)(ancestors)
    slot_token, slot_gate = jax.vmap(dispatch_all)(routes.reshape(groups, TOK_ROW, TOPK), gates.reshape(groups, TOK_ROW, TOPK))
    tree_shape = (NTREES, TREE, HEADS, HD)

    def forward(x_in, gain_one, query_w, key_w, value_w, gain_query, gain_key, out_w, gain_two, gate_w, up_w, down_w):
        scale_one = lax.rsqrt(lax.optimization_barrier(jnp.mean(x_in * x_in, -1, keepdims=True)) + EPS)
        normed_one = low(x_in * scale_one * gain_one)
        query = low_back(jnp.dot(normed_one, query_w, precision=HIGHEST))
        keyed = low_back(jnp.dot(normed_one, key_w, precision=HIGHEST))
        values = low(low_back(jnp.dot(normed_one, value_w, precision=HIGHEST)))
        q_normed = query * lax.rsqrt(lax.optimization_barrier(jnp.mean(query * query, -1, keepdims=True)) + EPS) * gain_query
        k_normed = keyed * lax.rsqrt(lax.optimization_barrier(jnp.mean(keyed * keyed, -1, keepdims=True)) + EPS) * gain_key
        q_rot = low(jax.vmap(rotate)(q_normed.reshape(tree_shape), cos_table, sin_table))
        k_rot = low(jax.vmap(rotate)(k_normed.reshape(tree_shape), cos_table, sin_table))
        attended = lax.map(jax.checkpoint(attend_tree), (q_rot, k_rot, values.reshape(tree_shape), ancestors))
        attended = low_back(low(attended.reshape(TOKENS, D)))
        residual = x_in + low_back(jnp.dot(attended, out_w.T, precision=HIGHEST))
        mid = low(residual)
        scale_two = lax.rsqrt(lax.optimization_barrier(jnp.mean(mid * mid, -1, keepdims=True)) + EPS)
        normed_two = low(mid * scale_two * gain_two)

        def group_step(parts):
            return group_experts(parts[0], parts[1], parts[2], gate_w, up_w, down_w)
        mixed = lax.map(jax.checkpoint(group_step), (normed_two.reshape(groups, TOK_ROW, D), slot_token, slot_gate))
        return residual + mixed.reshape(TOKENS, D)
    result, pullback = jax.vjp(forward, tokens.astype(jnp.float32), attn_norm.astype(jnp.float32), w_query.astype(jnp.float32), w_key.astype(jnp.float32), w_value.astype(jnp.float32), q_norm.astype(jnp.float32), k_norm.astype(jnp.float32), w_out.astype(jnp.float32), moe_norm.astype(jnp.float32), w_gate.astype(jnp.float32), w_up.astype(jnp.float32), w_down.astype(jnp.float32))
    grads = pullback(cotangent.astype(jnp.float32))
    return (result.astype(jnp.bfloat16), grads[0], grads[1], grads[2], grads[3], grads[4], grads[5], grads[6], grads[7], grads[8], grads[9], grads[10], grads[11])
```

```python
import math

import jax
import jax.numpy as jnp
from jax import lax
from jax.experimental import pallas as pl
from jax.experimental.pallas import tpu as pltpu
from jax.sharding import PartitionSpec as P

HD = 128
FF = 1024
SEG = 128
TREE = 2560
NSEG = 20
TRUNK = 512
BRANCH_END = 1024
LEAF_END = 2048
CAP = 426
CAPP = 432


EPS = 1e-05
NEGATIVE = -1e30
MIB = 1024 * 1024


def depths_of(parent_ids):
    segment_ids = jnp.arange(NSEG, dtype=jnp.int32)

    def advance(turn_index, loop_state):
        current, depth = loop_state
        matches = current[:, None] == segment_ids[None, :]
        parent_of = jnp.sum(jnp.where(matches, parent_ids[None, :], 0), 1)
        current = jnp.where(current >= 0, parent_of, -1)
        return (current, depth + (current >= 0).astype(jnp.int32))

    start = (segment_ids, jnp.zeros((NSEG,), jnp.int32))
    state = start
    for turn in range(6):
        state = advance(turn, state)
    return state[1]


def rope_tables(parent_ids):
    depths = depths_of(parent_ids)
    position = jnp.arange(TREE, dtype=jnp.int32)
    places = (jnp.repeat(depths, SEG) * SEG + position % SEG).astype(jnp.float32)
    frequency = jnp.exp(jnp.arange(HD // 2, dtype=jnp.float32) * (-2.0 * math.log(10000.0) / HD))
    angles = places[:, None] * frequency[None, :]
    cosine, sine = jnp.cos(angles), jnp.sin(angles)
    return (
        jnp.concatenate([cosine, cosine], -1),
        jnp.concatenate([-sine, sine], -1),
    )


def dot_f32(left, right, left_dim, right_dim):
    return lax.dot_general(
        left, right, (((left_dim,), (right_dim,)), ((), ())), preferred_element_type=jnp.float32
    )


def contract_rows(left, right):
    return dot_f32(left, right, 0, 0)


def contract_cols(left, right):
    return dot_f32(left, right, 1, 1)


def over_col(partial_value):
    return jnp.sum(lax.all_gather(partial_value, "col", axis=0), 0)


def causal(count):
    rows = lax.broadcasted_iota(jnp.int32, (count, count), 0)
    cols = lax.broadcasted_iota(jnp.int32, (count, count), 1)
    return cols <= rows


def key_starts(chunk, parent_of):
    first = chunk * 4
    blocks = [[(first + s) * SEG for s in range(4)]]
    if TRUNK * chunk >= BRANCH_END and TRUNK * chunk < LEAF_END:
        blocks.append([parent_of[first + s] * SEG for s in range(4)])
    return blocks


def seg_dot(rows, keys_ref, starts):
    return jnp.concatenate(
        [
            contract_cols(rows[s * SEG : (s + 1) * SEG], keys_ref[pl.ds(starts[s], SEG), :])
            for s in range(4)
        ],
        0,
    )


def chunk_weights(chunk, query, k_ref, blocks, scale):
    pieces = []
    if chunk == 0:
        score = contract_cols(query, k_ref[0:TRUNK, :]) * scale
        pieces.append(jnp.where(causal(TRUNK), score, NEGATIVE))
    else:
        if TRUNK * chunk < LEAF_END:
            pieces.append(contract_cols(query, k_ref[0:TRUNK, :]) * scale)
        mask = jnp.concatenate([causal(SEG)] * 4, 0)
        pieces.append(jnp.where(mask, seg_dot(query, k_ref, blocks[0]) * scale, NEGATIVE))
        for starts in blocks[1:]:
            pieces.append(seg_dot(query, k_ref, starts) * scale)
    highest = jnp.max(pieces[0], -1, keepdims=True)
    for piece in pieces[1:]:
        highest = jnp.maximum(highest, jnp.max(piece, -1, keepdims=True))
    raised = [jnp.exp(piece - highest) for piece in pieces]
    total = jnp.sum(raised[0], -1, keepdims=True)
    for piece in raised[1:]:
        total = total + jnp.sum(piece, -1, keepdims=True)
    inverse = 1.0 / total
    return [piece * inverse for piece in raised]


def chunk_parts(chunk, pieces, blocks):
    places = []
    if chunk == 0:
        places = [None]
    else:
        if TRUNK * chunk < LEAF_END:
            places.append(None)
        places = places + blocks
    return list(zip(pieces, places))


def forward_kernel(
    parents_ref,
    q_ref,
    k_ref,
    v_ref,
    qs_ref,
    ks_ref,
    qg_ref,
    kg_ref,
    cos_ref,
    sin_ref,
    att_ref,
    qr_ref,
    kr_ref,
    vl_ref,
):
    tree = pl.program_id(0)
    scale = 1.0 / math.sqrt(HD)
    parent_of = [parents_ref[tree, s] for s in range(NSEG)]

    def turned(field):
        return field * cos_ref[...] + pltpu.roll(field, HD // 2, 1) * sin_ref[...]

    qr_ref[...] = turned(q_ref[...] * qs_ref[...] * qg_ref[...]).astype(jnp.bfloat16)
    kr_ref[...] = turned(k_ref[...] * ks_ref[...] * kg_ref[...]).astype(jnp.bfloat16)
    vl_ref[...] = v_ref[...].astype(jnp.bfloat16)
    for chunk in range(TREE // TRUNK):
        rows = slice(chunk * TRUNK, (chunk + 1) * TRUNK)
        blocks = key_starts(chunk, parent_of)
        weights = chunk_weights(chunk, qr_ref[rows, :], kr_ref, blocks, scale)
        total = jnp.zeros((TRUNK, HD), jnp.float32)
        for weight, starts in chunk_parts(chunk, weights, blocks):
            low = weight.astype(jnp.bfloat16)
            if starts is None:
                total = total + dot_f32(low, vl_ref[0:TRUNK, :], 1, 0)
            else:
                total = total + jnp.concatenate(
                    [
                        dot_f32(
                            low[s * SEG : (s + 1) * SEG], vl_ref[pl.ds(starts[s], SEG), :], 1, 0
                        )
                        for s in range(4)
                    ],
                    0,
                )
        att_ref[rows, :] = total.astype(jnp.bfloat16)


def backward_kernel(
    parents_ref,
    qr_ref,
    kr_ref,
    vl_ref,
    do_ref,
    cos_ref,
    sin_ref,
    dq_ref,
    dk_ref,
    dv_ref,
    dv_acc,
):
    tree = pl.program_id(0)
    scale = 1.0 / math.sqrt(HD)
    parent_of = [parents_ref[tree, s] for s in range(NSEG)]
    dk_ref[...] = jnp.zeros_like(dk_ref)
    dv_acc[...] = jnp.zeros_like(dv_acc)
    for chunk in range(TREE // TRUNK):
        rows = slice(chunk * TRUNK, (chunk + 1) * TRUNK)
        blocks = key_starts(chunk, parent_of)
        query = qr_ref[rows, :]
        grad = do_ref[rows, :]
        weights = chunk_weights(chunk, query, kr_ref, blocks, scale)
        parts = chunk_parts(chunk, weights, blocks)
        d_weights = []
        row_dot = jnp.zeros((TRUNK, 1), jnp.float32)
        for weight, starts in parts:
            if starts is None:
                d_weight = contract_cols(grad, vl_ref[0:TRUNK, :])
            else:
                d_weight = seg_dot(grad, vl_ref, starts)
            d_weights.append(d_weight)
            row_dot = row_dot + jnp.sum(weight * d_weight, -1, keepdims=True)
        d_query = jnp.zeros((TRUNK, HD), jnp.float32)
        for (weight, starts), d_weight in zip(parts, d_weights):
            low = weight.astype(jnp.bfloat16)
            d_score = (weight * (d_weight - row_dot)).astype(jnp.bfloat16)
            if starts is None:
                d_query = d_query + dot_f32(d_score, kr_ref[0:TRUNK, :], 1, 0)
                dk_ref[0:TRUNK, :] += contract_rows(d_score, query)
                dv_acc[0:TRUNK, :] += contract_rows(low, grad)
            else:
                turns = []
                for s in range(4):
                    own = slice(s * SEG, (s + 1) * SEG)
                    keys = pl.ds(starts[s], SEG)
                    turns.append(dot_f32(d_score[own], kr_ref[keys, :], 1, 0))
                    dk_ref[keys, :] += contract_rows(d_score[own], query[own])
                    dv_acc[keys, :] += contract_rows(low[own], grad[own])
                d_query = d_query + jnp.concatenate(turns, 0)
        dq_ref[rows, :] = d_query

    def unturned(field):
        return (field * cos_ref[...] - pltpu.roll(field, HD // 2, 1) * sin_ref[...]) * scale

    dq_ref[...] = unturned(dq_ref[...])
    dk_ref[...] = unturned(dk_ref[...])
    dv_ref[...] = dv_acc[...].astype(jnp.bfloat16)


def attend(parents, qkv, q_scale, k_scale, q_gain, k_gain, cos_table, sin_table, heads):
    trees = parents.shape[0]
    rows = qkv.shape[0]

    def field(shift):
        return pl.BlockSpec((TREE, HD), lambda t, h, p: (t, h + shift))

    scale_spec = pl.BlockSpec((TREE, 1), lambda t, h, p: (t, 0))
    gain_spec = pl.BlockSpec((1, HD), lambda t, h, p: (0, h))
    table = pl.BlockSpec((TREE, HD), lambda t, h, p: (t, 0))
    return pl.pallas_call(
        forward_kernel,
        grid_spec=pltpu.PrefetchScalarGridSpec(
            num_scalar_prefetch=1,
            grid=(trees, heads),
            in_specs=[
                field(0),
                field(heads),
                field(2 * heads),
                scale_spec,
                scale_spec,
                gain_spec,
                gain_spec,
                table,
                table,
            ],
            out_specs=[field(0)] * 4,
        ),
        out_shape=[jax.ShapeDtypeStruct((rows, heads * HD), jnp.bfloat16)] * 4,
        compiler_params=pltpu.CompilerParams(vmem_limit_bytes=50 * MIB),
        name="tree_forward",
    )(
        parents,
        qkv,
        qkv,
        qkv,
        q_scale,
        k_scale,
        q_gain[None, :],
        k_gain[None, :],
        cos_table,
        sin_table,
    )


def attend_back(parents, q_rot, k_rot, values, d_attended, cos_table, sin_table, heads):
    trees = parents.shape[0]
    rows = q_rot.shape[0]
    field = pl.BlockSpec((TREE, HD), lambda t, h, p: (t, h))
    table = pl.BlockSpec((TREE, HD), lambda t, h, p: (t, 0))
    return pl.pallas_call(
        backward_kernel,
        grid_spec=pltpu.PrefetchScalarGridSpec(
            num_scalar_prefetch=1,
            grid=(trees, heads),
            in_specs=[field, field, field, field, table, table],
            out_specs=[field] * 3,
            scratch_shapes=[pltpu.VMEM((TREE, HD), jnp.float32)],
        ),
        out_shape=[
            jax.ShapeDtypeStruct((rows, heads * HD), jnp.float32),
            jax.ShapeDtypeStruct((rows, heads * HD), jnp.float32),
            jax.ShapeDtypeStruct((rows, heads * HD), jnp.bfloat16),
        ],
        compiler_params=pltpu.CompilerParams(vmem_limit_bytes=50 * MIB),
        name="tree_backward",
    )(parents, q_rot, k_rot, values, d_attended, cos_table, sin_table)


def combine_kernel(slot_ref, y_ref, out_ref):
    units = y_ref.shape[0]
    total = None
    for e in range(units):
        slots = lax.broadcasted_iota(jnp.int32, (slot_ref.shape[0], CAPP), 1)
        picks = (slot_ref[:, e : e + 1] == slots).astype(jnp.bfloat16)
        term = dot_f32(picks, y_ref[e, 0], 1, 0)
        total = term if total is None else total + term
    out_ref[...] = total.astype(out_ref.dtype)


def combine(slot_of, slot_rows, tok_rows):
    units, groups, _, width = slot_rows.shape
    block = 512
    steps = tok_rows // block
    return pl.pallas_call(
        combine_kernel,
        grid=(groups, steps),
        in_specs=[
            pl.BlockSpec((block, units), lambda g, t: (g * steps + t, 0)),
            pl.BlockSpec((units, 1, CAPP, width), lambda g, t: (0, g, 0, 0)),
        ],
        out_specs=pl.BlockSpec((block, width), lambda g, t: (g * steps + t, 0)),
        out_shape=jax.ShapeDtypeStruct((groups * tok_rows, width), jnp.bfloat16),
        compiler_params=pltpu.CompilerParams(vmem_limit_bytes=50 * MIB),
        cost_estimate=pl.CostEstimate(
            flops=2 * groups * tok_rows * units * CAPP * width,
            bytes_accessed=2 * groups * tok_rows * width,
            transcendentals=0,
        ),
        name="combine",
    )(slot_of, slot_rows)


def rows_home(weight):
    groups = lax.axis_size("row")
    here = lax.axis_index("row")
    depth, columns = weight.shape
    share = columns // groups
    whole = jnp.zeros((depth * groups, share), weight.dtype)
    for k in range(groups):
        to = (here + k) % groups
        block = lax.dynamic_slice_in_dim(weight, to * share, share, 1)
        if k > 0:
            block = lax.ppermute(block, "row", [(i, (i + k) % groups) for i in range(groups)])
        whole = lax.dynamic_update_slice_in_dim(
            whole, block, ((here - k) % groups) * depth, 0
        )
    return whole


def rows_back(grad):
    groups = lax.axis_size("row")
    here = lax.axis_index("row")
    depth, share = grad.shape[0] // groups, grad.shape[1]
    whole = jnp.zeros((depth, share * groups), jnp.float32)
    for k in range(groups):
        to = (here + k) % groups
        block = lax.dynamic_slice_in_dim(grad, to * depth, depth, 0)
        if k > 0:
            block = lax.ppermute(block, "row", [(i, (i + k) % groups) for i in range(groups)])
        whole = lax.dynamic_update_slice_in_dim(
            whole, block.astype(jnp.float32), ((here - k) % groups) * share, 1
        )
    return whole


def total_home(partial_rows):
    groups = lax.axis_size("row")
    here = lax.axis_index("row")
    part = lax.psum_scatter(partial_rows, "col", scatter_dimension=1, tiled=True)
    rows = part.shape[0] // groups
    total = None
    for k in range(groups):
        to = (here + k) % groups
        block = lax.dynamic_slice_in_dim(part, to * rows, rows, 0)
        if k > 0:
            block = lax.ppermute(block, "row", [(i, (i + k) % groups) for i in range(groups)])
        block = block.astype(jnp.float32)
        total = block if total is None else total + block
    return total


def gather_all(part_rows):
    return lax.all_gather(
        lax.all_gather(part_rows, "row", axis=0, tiled=True), "col", axis=1, tiled=True
    )


def body(
    tokens,
    attn_norm,
    w_query,
    w_key,
    w_value,
    q_norm,
    k_norm,
    w_out,
    moe_norm,
    w_gate,
    w_up,
    w_down,
    routes,
    gates,
    parents,
    cotangent,
):
    tok_rows, own_width = tokens.shape
    groups = lax.axis_size("row")
    cols = lax.axis_size("col")
    width = own_width * cols
    here, col = lax.axis_index("row"), lax.axis_index("col")
    col_start = col * own_width
    heads = own_width // HD
    trees = parents.shape[0]

    whole = lax.all_gather(tokens, "col", axis=1, tiled=True)
    qkv_cols = lax.all_gather(
        jnp.concatenate([w_query, w_key, w_value], 1), "row", axis=0, tiled=True
    )
    out_cols = lax.all_gather(w_out, "row", axis=0, tiled=True)
    cos_table, sin_table = jax.vmap(rope_tables)(parents)
    cos_table, sin_table = cos_table.reshape(-1, HD), sin_table.reshape(-1, HD)
    wide = whole.astype(jnp.float32)
    scale_one = lax.rsqrt(jnp.mean(wide * wide, 1, keepdims=True) + EPS)
    normed_one = (wide * scale_one * attn_norm[None, :]).astype(jnp.bfloat16)
    qkv = jnp.dot(normed_one, qkv_cols, preferred_element_type=jnp.float32)
    query, keyed = qkv[:, :own_width], qkv[:, own_width : 2 * own_width]
    squares = over_col(jnp.stack([jnp.sum(query * query, 1), jnp.sum(keyed * keyed, 1)]))
    q_scale = lax.rsqrt(squares[0] / width + EPS)[:, None]
    k_scale = lax.rsqrt(squares[1] / width + EPS)[:, None]
    q_gain = lax.dynamic_slice_in_dim(q_norm, col_start, own_width)
    k_gain = lax.dynamic_slice_in_dim(k_norm, col_start, own_width)
    attended, q_rot, k_rot, value_low = attend(
        parents, qkv, q_scale, k_scale, q_gain, k_gain, cos_table, sin_table, heads
    )
    attn_sum = lax.psum_scatter(
        contract_cols(attended, out_cols).astype(jnp.bfloat16),
        "col",
        scatter_dimension=1,
        tiled=True,
    )
    residual = tokens.astype(jnp.float32) + attn_sum.astype(jnp.float32)
    mid_low = residual.astype(jnp.bfloat16)
    mid_own = mid_low.astype(jnp.float32)
    mid_all = gather_all(mid_low)
    scale_two = lax.rsqrt(over_col(jnp.sum(mid_own * mid_own, 1)) / width + EPS)[:, None]

    share = w_gate.shape[1] // groups
    units, hidden_units = max(1, share // FF), min(share, FF)
    first_unit = col * (w_gate.shape[1] // FF) + (here * share) // FF
    route_all = lax.all_gather(routes, "row", axis=0)
    gate_all = lax.all_gather(gates, "row", axis=0)
    unit_ids = first_unit + jnp.arange(units, dtype=jnp.int32)
    match = route_all[None] == unit_ids[:, None, None, None]
    named = jnp.any(match, -1)
    token_gate = jnp.sum(jnp.where(match, gate_all[None], 0.0), -1)
    rank = jnp.cumsum(named.astype(jnp.int32), 2) - 1
    slot_of = jnp.where(named, rank, -1)
    in_slot = slot_of[:, :, None, :] == jnp.arange(CAPP, dtype=jnp.int32)[None, None, :, None]
    slot_token = jnp.sum(
        jnp.where(in_slot, jnp.arange(tok_rows, dtype=jnp.int32)[None, None, None, :], 0), -1
    )
    slot_gate = jnp.sum(jnp.where(in_slot, token_gate[:, :, None, :], 0.0), -1)
    slot_row = slot_token + (jnp.arange(groups, dtype=jnp.int32) * tok_rows)[None, :, None]
    slot_row = slot_row.reshape(-1)
    slot_gate = slot_gate.reshape(units, -1)[:, :, None]
    slot_of = slot_of.transpose(1, 2, 0).reshape(groups * tok_rows, units)

    gate_home, up_home, down_home = rows_home(w_gate), rows_home(w_up), rows_home(w_down)
    grad_all = gather_all(cotangent)
    slots = groups * CAPP
    slot_mid = mid_all[slot_row].astype(jnp.float32)
    slot_scale = lax.rsqrt(jnp.mean(slot_mid * slot_mid, 1, keepdims=True) + EPS)
    expert_in = (slot_mid * slot_scale * moe_norm[None, :]).astype(jnp.bfloat16)
    expert_in = expert_in.reshape(units, slots, width)
    slot_grad = grad_all[slot_row].astype(jnp.float32).reshape(units, slots, width)
    d_out = (slot_gate * slot_grad).astype(jnp.bfloat16)

    gated, d_in, gate_grads, up_grads, down_grads = [], [], [], [], []
    for e in range(units):
        unit = slice(e * hidden_units, (e + 1) * hidden_units)
        x_e, d_e = expert_in[e], d_out[e]
        gate_w, up_w, down_w = gate_home[:, unit], up_home[:, unit], down_home[:, unit]
        gate_act = dot_f32(x_e, gate_w, 1, 0)
        up_act = dot_f32(x_e, up_w, 1, 0)
        sigmoid_gate = jax.nn.sigmoid(gate_act)
        silu_gate = gate_act * sigmoid_gate
        hidden = (silu_gate * up_act).astype(jnp.bfloat16)
        down_grads.append(contract_rows(d_e, hidden).astype(jnp.bfloat16))
        d_hidden = dot_f32(d_e, down_w, 1, 0)
        d_gate = (
            d_hidden * up_act * sigmoid_gate * (1.0 + gate_act * (1.0 - sigmoid_gate))
        ).astype(jnp.bfloat16)
        d_up = (d_hidden * silu_gate).astype(jnp.bfloat16)
        d_in.append(
            (contract_cols(d_gate, gate_w) + contract_cols(d_up, up_w)).astype(jnp.bfloat16)
        )
        gate_grads.append(contract_rows(x_e, d_gate).astype(jnp.bfloat16))
        up_grads.append(contract_rows(x_e, d_up).astype(jnp.bfloat16))
        gated.append((slot_gate[e] * contract_cols(hidden, down_w)).astype(jnp.bfloat16))
    slot_shape = (units, groups, CAPP, width)
    d_normed_two = total_home(combine(slot_of, jnp.stack(d_in).reshape(slot_shape), tok_rows))
    moe_sum = total_home(combine(slot_of, jnp.stack(gated).reshape(slot_shape), tok_rows))
    output = (residual + moe_sum).astype(jnp.bfloat16)
    w_down_grad = rows_back(jnp.concatenate(down_grads, 1))
    w_gate_grad = rows_back(jnp.concatenate(gate_grads, 1))
    w_up_grad = rows_back(jnp.concatenate(up_grads, 1))

    gain_two = lax.dynamic_slice_in_dim(moe_norm, col_start, own_width)
    moe_dot = over_col(jnp.sum(d_normed_two * gain_two * mid_own, 1))
    d_residual = (
        cotangent.astype(jnp.float32)
        + scale_two * gain_two * d_normed_two
        - mid_own * scale_two**3 * (moe_dot / width)[:, None]
    )
    moe_gain_grad = jnp.sum(d_normed_two * mid_own * scale_two, 0)
    d_attn_whole = lax.all_gather(d_residual.astype(jnp.bfloat16), "col", axis=1, tiled=True)
    d_attended = jnp.dot(d_attn_whole, out_cols, preferred_element_type=jnp.float32).astype(
        jnp.bfloat16
    )
    d_qn, d_kn, d_values = attend_back(
        parents, q_rot, k_rot, value_low, d_attended, cos_table, sin_table, heads
    )
    qk_dots = over_col(
        jnp.stack([jnp.sum(query * q_gain * d_qn, 1), jnp.sum(keyed * k_gain * d_kn, 1)])
    )
    d_query = (
        q_scale * q_gain * d_qn - query * q_scale**3 * (qk_dots[0] / width)[:, None]
    ).astype(jnp.bfloat16)
    d_keyed = (
        k_scale * k_gain * d_kn - keyed * k_scale**3 * (qk_dots[1] / width)[:, None]
    ).astype(jnp.bfloat16)
    q_gain_grad = jnp.sum(d_qn * query * q_scale, 0)
    k_gain_grad = jnp.sum(d_kn * keyed * k_scale, 0)
    d_qkv = jnp.concatenate([d_query, d_keyed, d_values], 1)
    d_normed_one = lax.psum_scatter(
        contract_cols(d_qkv, qkv_cols).astype(jnp.bfloat16),
        "col",
        scatter_dimension=1,
        tiled=True,
    ).astype(jnp.float32)
    attn_grads = lax.psum_scatter(
        jnp.concatenate(
            [contract_rows(normed_one, d_qkv), contract_rows(d_attn_whole, attended)], 1
        ).astype(jnp.bfloat16),
        "row",
        scatter_dimension=0,
        tiled=True,
    ).astype(jnp.float32)
    w_query_grad = attn_grads[:, :own_width]
    w_key_grad = attn_grads[:, own_width : 2 * own_width]
    w_value_grad = attn_grads[:, 2 * own_width : 3 * own_width]
    w_out_grad = attn_grads[:, 3 * own_width :]
    tokens_own = tokens.astype(jnp.float32)
    gain_one = lax.dynamic_slice_in_dim(attn_norm, col_start, own_width)
    attn_dot = over_col(jnp.sum(d_normed_one * gain_one * tokens_own, 1))
    tokens_grad = (
        d_residual
        + scale_one * gain_one * d_normed_one
        - tokens_own * scale_one**3 * (attn_dot / width)[:, None]
    )
    attn_gain_grad = jnp.sum(d_normed_one * tokens_own * scale_one, 0)
    gain_grads = jnp.sum(
        lax.all_gather(
            jnp.stack([attn_gain_grad, q_gain_grad, k_gain_grad, moe_gain_grad]), "row", axis=0
        ),
        0,
    )
    return (
        output,
        tokens_grad,
        gain_grads[0],
        w_query_grad,
        w_key_grad,
        w_value_grad,
        gain_grads[1],
        gain_grads[2],
        w_out_grad,
        gain_grads[3],
        w_gate_grad,
        w_up_grad,
        w_down_grad,
    )


def solution(mesh):
    grid = P("row", "col")
    rows = P("row", None)
    in_specs = (
        grid,
        P(),
        grid,
        grid,
        grid,
        P(),
        P(),
        grid,
        P(),
        grid,
        grid,
        grid,
        rows,
        rows,
        rows,
        grid,
    )
    out_specs = (
        grid,
        grid,
        P("col"),
        grid,
        grid,
        grid,
        P("col"),
        P("col"),
        grid,
        P("col"),
        grid,
        grid,
        grid,
    )
    return jax.shard_map(body, mesh=mesh, in_specs=in_specs, out_specs=out_specs, check_vma=False)
```

```python
import functools
import math

import jax
import jax.numpy as jnp
from jax import lax
from jax.experimental import pallas as pl
from jax.experimental.pallas import tpu as pltpu
from jax.sharding import PartitionSpec as P

HD = 128
FF = 1024
SEG = 128
TREE = 2560
NSEG = 20
TRUNK = 512
BRANCH_END = 1024
LEAF_END = 2048
CAP = 426
CAPP = 432


EPS = 1e-05
NEGATIVE = -1e30
MIB = 1024 * 1024


def depths_of(parent_ids):
    segment_ids = jnp.arange(NSEG, dtype=jnp.int32)

    def advance(turn_index, loop_state):
        current, depth = loop_state
        matches = current[:, None] == segment_ids[None, :]
        parent_of = jnp.sum(jnp.where(matches, parent_ids[None, :], 0), 1)
        current = jnp.where(current >= 0, parent_of, -1)
        return (current, depth + (current >= 0).astype(jnp.int32))

    start = (segment_ids, jnp.zeros((NSEG,), jnp.int32))
    state = start
    for turn in range(6):
        state = advance(turn, state)
    return state[1]


def rope_tables(parent_ids):
    depths = depths_of(parent_ids)
    position = jnp.arange(TREE, dtype=jnp.int32)
    places = (jnp.repeat(depths, SEG) * SEG + position % SEG).astype(jnp.float32)
    frequency = jnp.exp(jnp.arange(HD // 2, dtype=jnp.float32) * (-2.0 * math.log(10000.0) / HD))
    angles = places[:, None] * frequency[None, :]
    cosine, sine = jnp.cos(angles), jnp.sin(angles)
    return (
        jnp.concatenate([cosine, cosine], -1),
        jnp.concatenate([-sine, sine], -1),
    )


def dot_f32(left, right, left_dim, right_dim):
    return lax.dot_general(
        left, right, (((left_dim,), (right_dim,)), ((), ())), preferred_element_type=jnp.float32
    )


def contract_rows(left, right):
    return dot_f32(left, right, 0, 0)


def contract_cols(left, right):
    return dot_f32(left, right, 1, 1)


def over_col(partial_value):
    return jnp.sum(lax.all_gather(partial_value, "col", axis=0), 0)


def after(value, *earlier):
    return lax.optimization_barrier((value,) + earlier)[0]


def gather_blocks(part):
    count = lax.axis_size("col")

    def swap(block, bits):
        return lax.ppermute(block, "col", [(i, i ^ bits) for i in range(count)])

    if count == 8:
        half = part.shape[0] // 2
        side, far, twin = swap(part, 2), swap(part, 4), swap(part, 1)
        corner = jnp.concatenate([swap(far[:half], 2), swap(side[half:], 4)], 0)
        return [
            part,
            twin,
            side,
            swap(side, 1),
            far,
            swap(far, 1),
            corner,
            swap(corner, 1),
        ]
    blocks = [part]
    bits = 1
    while bits < count:
        blocks = blocks + [swap(block, bits) for block in blocks]
        bits = bits * 2
    return blocks


def block_order(rows, depth):
    own = lax.axis_index("col")
    count = rows.shape[0] // depth
    return jnp.concatenate(
        [lax.dynamic_slice_in_dim(rows, (own ^ k) * depth, depth, 0) for k in range(count)], 0
    )


def causal(count):
    rows = lax.broadcasted_iota(jnp.int32, (count, count), 0)
    cols = lax.broadcasted_iota(jnp.int32, (count, count), 1)
    return cols <= rows


def key_starts(chunk, parent_of):
    first = chunk * 4
    blocks = [[(first + s) * SEG for s in range(4)]]
    if TRUNK * chunk >= BRANCH_END and TRUNK * chunk < LEAF_END:
        blocks.append([parent_of[first + s] * SEG for s in range(4)])
    return blocks


def seg_dot(rows, keys_ref, starts):
    return jnp.concatenate(
        [
            contract_cols(rows[s * SEG : (s + 1) * SEG], keys_ref[pl.ds(starts[s], SEG), :])
            for s in range(4)
        ],
        0,
    )


def chunk_weights(chunk, query, k_ref, blocks, scale):
    pieces = []
    if chunk == 0:
        score = contract_cols(query, k_ref[0:TRUNK, :]) * scale
        pieces.append(jnp.where(causal(TRUNK), score, NEGATIVE))
    else:
        if TRUNK * chunk < LEAF_END:
            pieces.append(contract_cols(query, k_ref[0:TRUNK, :]) * scale)
        mask = jnp.concatenate([causal(SEG)] * 4, 0)
        pieces.append(jnp.where(mask, seg_dot(query, k_ref, blocks[0]) * scale, NEGATIVE))
        for starts in blocks[1:]:
            pieces.append(seg_dot(query, k_ref, starts) * scale)
    highest = jnp.max(pieces[0], -1, keepdims=True)
    for piece in pieces[1:]:
        highest = jnp.maximum(highest, jnp.max(piece, -1, keepdims=True))
    raised = [jnp.exp(piece - highest) for piece in pieces]
    total = jnp.sum(raised[0], -1, keepdims=True)
    for piece in raised[1:]:
        total = total + jnp.sum(piece, -1, keepdims=True)
    inverse = 1.0 / total
    return [piece * inverse for piece in raised]


def chunk_parts(chunk, pieces, blocks):
    places = []
    if chunk == 0:
        places = [None]
    else:
        if TRUNK * chunk < LEAF_END:
            places.append(None)
        places = places + blocks
    return list(zip(pieces, places))


def forward_kernel(
    parents_ref,
    q_ref,
    k_ref,
    v_ref,
    qs_ref,
    ks_ref,
    qg_ref,
    kg_ref,
    cos_ref,
    sin_ref,
    att_ref,
    qr_ref,
    kr_ref,
    vl_ref,
):
    tree = pl.program_id(0)
    scale = 1.0 / math.sqrt(HD)
    parent_of = [parents_ref[tree, s] for s in range(NSEG)]

    def turned(field):
        return field * cos_ref[...] + pltpu.roll(field, HD // 2, 1) * sin_ref[...]

    qr_ref[...] = turned(q_ref[...] * qs_ref[...] * qg_ref[...]).astype(jnp.bfloat16)
    kr_ref[...] = turned(k_ref[...] * ks_ref[...] * kg_ref[...]).astype(jnp.bfloat16)
    vl_ref[...] = v_ref[...].astype(jnp.bfloat16)
    for chunk in range(TREE // TRUNK):
        rows = slice(chunk * TRUNK, (chunk + 1) * TRUNK)
        blocks = key_starts(chunk, parent_of)
        weights = chunk_weights(chunk, qr_ref[rows, :], kr_ref, blocks, scale)
        total = jnp.zeros((TRUNK, HD), jnp.float32)
        for weight, starts in chunk_parts(chunk, weights, blocks):
            low = weight.astype(jnp.bfloat16)
            if starts is None:
                total = total + dot_f32(low, vl_ref[0:TRUNK, :], 1, 0)
            else:
                total = total + jnp.concatenate(
                    [
                        dot_f32(
                            low[s * SEG : (s + 1) * SEG], vl_ref[pl.ds(starts[s], SEG), :], 1, 0
                        )
                        for s in range(4)
                    ],
                    0,
                )
        att_ref[rows, :] = total.astype(jnp.bfloat16)


def backward_kernel(
    parents_ref,
    qr_ref,
    kr_ref,
    vl_ref,
    do_ref,
    cos_ref,
    sin_ref,
    dq_ref,
    dk_ref,
    dv_ref,
    dv_acc,
):
    tree = pl.program_id(0)
    scale = 1.0 / math.sqrt(HD)
    parent_of = [parents_ref[tree, s] for s in range(NSEG)]
    dk_ref[...] = jnp.zeros_like(dk_ref)
    dv_acc[...] = jnp.zeros_like(dv_acc)
    for chunk in range(TREE // TRUNK):
        rows = slice(chunk * TRUNK, (chunk + 1) * TRUNK)
        blocks = key_starts(chunk, parent_of)
        query = qr_ref[rows, :]
        grad = do_ref[rows, :]
        weights = chunk_weights(chunk, query, kr_ref, blocks, scale)
        parts = chunk_parts(chunk, weights, blocks)
        d_weights = []
        row_dot = jnp.zeros((TRUNK, 1), jnp.float32)
        for weight, starts in parts:
            if starts is None:
                d_weight = contract_cols(grad, vl_ref[0:TRUNK, :])
            else:
                d_weight = seg_dot(grad, vl_ref, starts)
            d_weights.append(d_weight)
            row_dot = row_dot + jnp.sum(weight * d_weight, -1, keepdims=True)
        d_query = jnp.zeros((TRUNK, HD), jnp.float32)
        for (weight, starts), d_weight in zip(parts, d_weights):
            low = weight.astype(jnp.bfloat16)
            d_score = (weight * (d_weight - row_dot)).astype(jnp.bfloat16)
            if starts is None:
                d_query = d_query + dot_f32(d_score, kr_ref[0:TRUNK, :], 1, 0)
                dk_ref[0:TRUNK, :] += contract_rows(d_score, query)
                dv_acc[0:TRUNK, :] += contract_rows(low, grad)
            else:
                turns = []
                for s in range(4):
                    own = slice(s * SEG, (s + 1) * SEG)
                    keys = pl.ds(starts[s], SEG)
                    turns.append(dot_f32(d_score[own], kr_ref[keys, :], 1, 0))
                    dk_ref[keys, :] += contract_rows(d_score[own], query[own])
                    dv_acc[keys, :] += contract_rows(low[own], grad[own])
                d_query = d_query + jnp.concatenate(turns, 0)
        dq_ref[rows, :] = d_query

    def unturned(field):
        return (field * cos_ref[...] - pltpu.roll(field, HD // 2, 1) * sin_ref[...]) * scale

    dq_ref[...] = unturned(dq_ref[...])
    dk_ref[...] = unturned(dk_ref[...])
    dv_ref[...] = dv_acc[...].astype(jnp.bfloat16)


def attend(parents, qkv, q_scale, k_scale, q_gain, k_gain, cos_table, sin_table, heads):
    trees = parents.shape[0]
    rows = qkv.shape[0]

    def field(shift):
        return pl.BlockSpec((TREE, HD), lambda t, h, p: (t, h + shift))

    scale_spec = pl.BlockSpec((TREE, 1), lambda t, h, p: (t, 0))
    gain_spec = pl.BlockSpec((1, HD), lambda t, h, p: (0, h))
    table = pl.BlockSpec((TREE, HD), lambda t, h, p: (t, 0))
    return pl.pallas_call(
        forward_kernel,
        grid_spec=pltpu.PrefetchScalarGridSpec(
            num_scalar_prefetch=1,
            grid=(trees, heads),
            in_specs=[
                field(0),
                field(heads),
                field(2 * heads),
                scale_spec,
                scale_spec,
                gain_spec,
                gain_spec,
                table,
                table,
            ],
            out_specs=[field(0)] * 4,
        ),
        out_shape=[jax.ShapeDtypeStruct((rows, heads * HD), jnp.bfloat16)] * 4,
        compiler_params=pltpu.CompilerParams(vmem_limit_bytes=50 * MIB),
        name="tree_forward",
    )(
        parents,
        qkv,
        qkv,
        qkv,
        q_scale,
        k_scale,
        q_gain[None, :],
        k_gain[None, :],
        cos_table,
        sin_table,
    )


def attend_back(parents, q_rot, k_rot, values, d_attended, cos_table, sin_table, heads):
    trees = parents.shape[0]
    rows = q_rot.shape[0]
    field = pl.BlockSpec((TREE, HD), lambda t, h, p: (t, h))
    table = pl.BlockSpec((TREE, HD), lambda t, h, p: (t, 0))
    return pl.pallas_call(
        backward_kernel,
        grid_spec=pltpu.PrefetchScalarGridSpec(
            num_scalar_prefetch=1,
            grid=(trees, heads),
            in_specs=[field, field, field, field, table, table],
            out_specs=[field] * 3,
            scratch_shapes=[pltpu.VMEM((TREE, HD), jnp.float32)],
        ),
        out_shape=[
            jax.ShapeDtypeStruct((rows, heads * HD), jnp.float32),
            jax.ShapeDtypeStruct((rows, heads * HD), jnp.float32),
            jax.ShapeDtypeStruct((rows, heads * HD), jnp.bfloat16),
        ],
        compiler_params=pltpu.CompilerParams(vmem_limit_bytes=50 * MIB),
        name="tree_backward",
    )(parents, q_rot, k_rot, values, d_attended, cos_table, sin_table)


def slots_kernel(slot_ref, gate_ref, gain_ref, x_ref, *refs, normed):
    units = slot_ref.shape[1]
    outs, gate_out, acc, gate_acc = refs[:units], refs[units], refs[units + 1], refs[units + 2]
    step = pl.program_id(1)

    @pl.when(step == 0)
    def _():
        acc[...] = jnp.zeros_like(acc)
        gate_acc[...] = jnp.zeros_like(gate_acc)

    for e in range(units):
        slots = lax.broadcasted_iota(jnp.int32, (CAPP, x_ref.shape[0]), 0)
        picks = slot_ref[0, e : e + 1, :] == slots
        acc[e] += dot_f32(picks.astype(jnp.bfloat16), x_ref[...], 1, 0)
        gate_acc[e] += jnp.sum(jnp.where(picks, gate_ref[0, e : e + 1, :], 0.0), 1, keepdims=True)

    @pl.when(step == pl.num_programs(1) - 1)
    def _():
        for e in range(units):
            rows = acc[e]
            if normed:
                scale = lax.rsqrt(jnp.mean(rows * rows, 1, keepdims=True) + EPS)
                outs[e][...] = (rows * scale * gain_ref[...]).astype(jnp.bfloat16)
            else:
                outs[e][...] = (gate_acc[e] * rows).astype(jnp.bfloat16)
            gate_out[e] = gate_acc[e]


def to_slots(slot_of, token_gate, gain, rows, normed):
    groups, units, tok_rows = slot_of.shape
    width = rows.shape[1]
    block = tok_rows // 2
    steps = tok_rows // block
    table = pl.BlockSpec((1, units, block), lambda g, t: (g, 0, t))
    out = pl.pallas_call(
        functools.partial(slots_kernel, normed=normed),
        grid=(groups, steps),
        in_specs=[
            table,
            table,
            pl.BlockSpec((1, width), lambda g, t: (0, 0)),
            pl.BlockSpec((block, width), lambda g, t: (g * steps + t, 0)),
        ],
        out_specs=[pl.BlockSpec((CAPP, width), lambda g, t: (g, 0))] * units
        + [pl.BlockSpec((units, CAPP, 1), lambda g, t: (0, g, 0))],
        out_shape=[jax.ShapeDtypeStruct((groups * CAPP, width), jnp.bfloat16)] * units
        + [jax.ShapeDtypeStruct((units, groups * CAPP, 1), jnp.float32)],
        scratch_shapes=[
            pltpu.VMEM((units, CAPP, width), jnp.float32),
            pltpu.VMEM((units, CAPP, 1), jnp.float32),
        ],
        compiler_params=pltpu.CompilerParams(vmem_limit_bytes=56 * MIB),
        cost_estimate=pl.CostEstimate(
            flops=2 * groups * tok_rows * units * CAPP * width,
            bytes_accessed=2 * groups * tok_rows * width,
            transcendentals=0,
        ),
        name="slots",
    )(slot_of, token_gate, gain[None, :], rows)
    return out[:units], out[units]


def combine_kernel(slot_ref, *refs):
    out_ref = refs[-1]
    total = None
    for e, y_ref in enumerate(refs[:-1]):
        slots = lax.broadcasted_iota(jnp.int32, (slot_ref.shape[0], CAPP), 1)
        picks = (slot_ref[:, e : e + 1] == slots).astype(jnp.bfloat16)
        term = dot_f32(picks, y_ref[0], 1, 0)
        total = term if total is None else total + term
    out_ref[...] = total.astype(out_ref.dtype)


def combine(slot_of, slot_rows, tok_rows, half=None):
    units, width = len(slot_rows), slot_rows[0].shape[1]
    groups = slot_rows[0].shape[0] // CAPP
    block = tok_rows // 4
    steps = 4 if half is None else 2
    first = 0 if half is None else 2 * half
    rows_spec = pl.BlockSpec((1, CAPP, width), lambda g, t: (g, 0, 0))
    return pl.pallas_call(
        combine_kernel,
        grid=(groups, steps),
        in_specs=[pl.BlockSpec((block, units), lambda g, t: (g * 4 + first + t, 0))]
        + [rows_spec] * units,
        out_specs=pl.BlockSpec((block, width), lambda g, t: (g * steps + t, 0)),
        out_shape=jax.ShapeDtypeStruct((groups * steps * block, width), jnp.bfloat16),
        compiler_params=pltpu.CompilerParams(vmem_limit_bytes=50 * MIB),
        cost_estimate=pl.CostEstimate(
            flops=2 * groups * steps * block * units * CAPP * width,
            bytes_accessed=2 * groups * steps * block * width,
            transcendentals=0,
        ),
        name="combine",
    )(slot_of, *[rows.reshape(groups, CAPP, width) for rows in slot_rows])


def shift_row(block, k):
    count = lax.axis_size("row")
    return lax.ppermute(block, "row", [(i, (i + k) % count) for i in range(count)])


def row_stack(part, *earlier):
    count = lax.axis_size("row")
    here = lax.axis_index("row")
    part = after(part, *earlier)
    whole = jnp.zeros((count,) + part.shape, part.dtype)
    for k in range(count):
        block = part if k == 0 else shift_row(part, k)
        whole = lax.dynamic_update_slice_in_dim(whole, block[None], (here - k) % count, 0)
    return whole


def crossing_units():
    count = lax.axis_size("row")
    units = []
    for k in range(1, count):
        parts = 1 if k in (1, count - 1) else 2
        units = units + [(k, part, parts) for part in range(parts)]
    return units


def home_unit(weight, unit, *earlier):
    k, part, parts = unit
    groups = lax.axis_size("row")
    share = weight.shape[1] // groups
    to = (lax.axis_index("row") + k) % groups
    block = lax.dynamic_slice_in_dim(
        after(weight, *earlier), to * share + part * (share // parts), share // parts, 1
    )
    return shift_row(block, k)


def at_home(weight, units, blocks):
    groups = lax.axis_size("row")
    here = lax.axis_index("row")
    depth, columns = weight.shape
    share = columns // groups
    own = lax.dynamic_slice_in_dim(weight, here * share, share, 1)
    whole = jnp.zeros((depth * groups, share), weight.dtype)
    whole = lax.dynamic_update_slice(whole, own, (here * depth, 0))
    for (k, part, parts), block in zip(units, blocks):
        row = ((here - k) % groups) * depth
        whole = lax.dynamic_update_slice(whole, block, (row, part * (share // parts)))
    return whole


def back_units(count):
    rows = lax.axis_size("row")
    units = []
    for k in range(1, rows):
        if k in (1, rows - 1):
            units.append((k, tuple(range(count))))
        else:
            units = units + [(k, (e,)) for e in range(count)]
    return units


def back_unit(grads, unit, *earlier):
    k, which = unit
    groups = lax.axis_size("row")
    depth = grads[0].shape[0] // groups
    to = (lax.axis_index("row") + k) % groups
    chosen = after([grads[e] for e in which], *earlier)
    return [
        shift_row(lax.dynamic_slice_in_dim(grad, to * depth, depth, 0), k) for grad in chosen
    ]


def at_owner(grads, units, received):
    groups = lax.axis_size("row")
    here = lax.axis_index("row")
    depth, hidden = grads[0].shape[0] // groups, grads[0].shape[1]
    share = hidden * len(grads)
    whole = jnp.zeros((depth, share * groups), jnp.float32)
    for e, grad in enumerate(grads):
        own = lax.dynamic_slice_in_dim(grad, here * depth, depth, 0).astype(jnp.float32)
        whole = lax.dynamic_update_slice(whole, own, (0, here * share + e * hidden))
    for (k, which), blocks in zip(units, received):
        for e, block in zip(which, blocks):
            start = ((here - k) % groups) * share + e * hidden
            whole = lax.dynamic_update_slice(whole, block.astype(jnp.float32), (0, start))
    return whole


def line_steps(part, *earlier):
    count = lax.axis_size("row")
    upward = downward = part
    steps = []
    for _ in range(count - 1):
        upward, downward = after((upward, downward), *earlier)
        upward = lax.ppermute(upward, "row", [(i, i + 1) for i in range(count - 1)])
        downward = lax.ppermute(downward, "row", [(i + 1, i) for i in range(count - 1)])
        earlier = (upward, downward)
        steps.append((upward, downward))
    return steps


def line_gather(part, steps):
    count = lax.axis_size("row")
    here = lax.axis_index("row")
    rows = part.shape[0]
    whole = jnp.zeros((rows * count, part.shape[1]), part.dtype)
    whole = lax.dynamic_update_slice_in_dim(whole, part, here * rows, 0)
    for k in range(1, count):
        block = jnp.where(here >= k, steps[k - 1][0], steps[count - k - 1][1])
        whole = lax.dynamic_update_slice_in_dim(whole, block, ((here - k) % count) * rows, 0)
    return whole


def group_total(part):
    groups = lax.axis_size("row")
    here = lax.axis_index("row")
    rows = part.shape[0] // groups
    total = None
    for k in range(groups):
        to = (here + k) % groups
        block = lax.dynamic_slice_in_dim(part, to * rows, rows, 0)
        if k > 0:
            block = lax.ppermute(block, "row", [(i, (i + k) % groups) for i in range(groups)])
        block = block.astype(jnp.float32)
        total = block if total is None else total + block
    return total


def body(
    tokens,
    attn_norm,
    w_query,
    w_key,
    w_value,
    q_norm,
    k_norm,
    w_out,
    moe_norm,
    w_gate,
    w_up,
    w_down,
    routes,
    gates,
    parents,
    cotangent,
):
    tok_rows, own_width = tokens.shape
    groups = lax.axis_size("row")
    cols = lax.axis_size("col")
    width = own_width * cols
    here, col = lax.axis_index("row"), lax.axis_index("col")
    col_start = col * own_width
    heads = own_width // HD
    trees = parents.shape[0]

    qkv_cols = lax.all_gather(
        jnp.concatenate([w_query, w_key, w_value], 1), "row", axis=0, tiled=True
    )
    out_cols = lax.all_gather(after(w_out, qkv_cols), "row", axis=0, tiled=True)
    shifts = crossing_units()
    last = len(shifts) - 1
    gate_units = [home_unit(w_gate, shifts[0], out_cols)]
    route_all, gate_all = row_stack(routes.T, out_cols), row_stack(gates.T, out_cols)

    wide = jnp.concatenate(gather_blocks(tokens), 1).astype(jnp.float32)
    cos_table, sin_table = jax.vmap(rope_tables)(parents)
    cos_table, sin_table = cos_table.reshape(-1, HD), sin_table.reshape(-1, HD)
    scale_one = lax.rsqrt(jnp.mean(wide * wide, 1, keepdims=True) + EPS)
    norm_gain = block_order(attn_norm, own_width)
    normed_one = (wide * scale_one * norm_gain[None, :]).astype(jnp.bfloat16)
    qkv_cols = block_order(qkv_cols, own_width)
    qkv = jnp.dot(normed_one, qkv_cols, preferred_element_type=jnp.float32)
    query, keyed = qkv[:, :own_width], qkv[:, own_width : 2 * own_width]
    squares = over_col(jnp.stack([jnp.sum(query * query, 1), jnp.sum(keyed * keyed, 1)]))
    q_scale = lax.rsqrt(squares[0] / width + EPS)[:, None]
    k_scale = lax.rsqrt(squares[1] / width + EPS)[:, None]
    q_gain = lax.dynamic_slice_in_dim(q_norm, col_start, own_width)
    k_gain = lax.dynamic_slice_in_dim(k_norm, col_start, own_width)
    q_scale = after(q_scale, gate_units[0])
    gate_units.append(home_unit(w_gate, shifts[1], gate_units[0]))
    attended, q_rot, k_rot, value_low = attend(
        parents, qkv, q_scale, k_scale, q_gain, k_gain, cos_table, sin_table, heads
    )
    attn_sum = lax.psum_scatter(
        after(contract_cols(attended, out_cols).astype(jnp.bfloat16), gate_units[1]),
        "col",
        scatter_dimension=1,
        tiled=True,
    )
    for unit in shifts[2:]:
        gate_units.append(home_unit(w_gate, unit, gate_units[1]))
    attn_sum = after(attn_sum, gate_units, route_all, gate_all)
    residual = tokens.astype(jnp.float32) + attn_sum.astype(jnp.float32)
    mid_low = residual.astype(jnp.bfloat16)
    mid_own = mid_low.astype(jnp.float32)
    mid_row = lax.all_gather(mid_low, "row", axis=0, tiled=True)

    share = w_gate.shape[1] // groups
    units, hidden_units = max(1, share // FF), min(share, FF)
    first_unit = col * (w_gate.shape[1] // FF) + (here * share) // FF
    unit_ids = first_unit + jnp.arange(units, dtype=jnp.int32)
    match = route_all[None] == unit_ids[:, None, None, None]
    named = jnp.any(match, 2)
    token_gate = jnp.sum(jnp.where(match, gate_all[None], 0.0), 2)
    rank = jnp.cumsum(named.astype(jnp.int32), 2) - 1
    slot_of = jnp.where(named, rank, -1)
    slot_of, token_gate = slot_of.transpose(1, 0, 2), token_gate.transpose(1, 0, 2)
    slot_column = slot_of.transpose(0, 2, 1).reshape(groups * tok_rows, units)
    gate_home = at_home(w_gate, shifts, gate_units)
    mid_row, slot_of, token_gate, slot_column, gate_home = after(
        (mid_row, slot_of, token_gate, slot_column, gate_home)
    )
    mid_all = lax.all_gather(mid_row, "col", axis=1, tiled=True)
    scale_two = lax.rsqrt(over_col(jnp.sum(mid_own * mid_own, 1)) / width + EPS)[:, None]
    grad_steps = line_steps(cotangent, mid_row)
    grad_row = line_gather(cotangent, grad_steps)
    up_units = [home_unit(w_up, shifts[0], grad_steps[-1])]
    for unit in shifts[1:last]:
        up_units.append(home_unit(w_up, unit, up_units[-1]))
    mid_all = after(mid_all, up_units[-2])
    grad_all = lax.all_gather(after(grad_row, mid_all), "col", axis=1, tiled=True)

    experts = range(units)
    cut = [slice(e * hidden_units, (e + 1) * hidden_units) for e in experts]
    expert_in, slot_gate = to_slots(slot_of, token_gate, moe_norm, mid_all, True)
    expert_in = after(expert_in, up_units[-1])
    up_units = after(up_units, expert_in)
    up_units.append(home_unit(w_up, shifts[last], up_units[-1], expert_in))
    gate_acts = [dot_f32(expert_in[e], gate_home[:, cut[e]], 1, 0) for e in experts]
    up_home, gate_acts = after((at_home(w_up, shifts, up_units), gate_acts))
    down_units = [home_unit(w_down, shifts[0], up_home)]
    acts = []
    for e in experts:
        up_act = dot_f32(expert_in[e], up_home[:, cut[e]], 1, 0)
        sigmoid_gate = jax.nn.sigmoid(gate_acts[e])
        silu_gate = gate_acts[e] * sigmoid_gate
        hidden = (silu_gate * up_act).astype(jnp.bfloat16)
        acts.append((gate_acts[e], up_act, sigmoid_gate, silu_gate, hidden))
    hiddens = after([act[-1] for act in acts], down_units[0])
    for unit in shifts[1:last]:
        down_units.append(home_unit(w_down, unit, down_units[-1], hiddens))
    grad_all = after(grad_all, down_units[-1])
    down_units.append(home_unit(w_down, shifts[last], grad_all))
    d_out, _ = to_slots(slot_of, token_gate, moe_norm, grad_all, False)
    d_out = after(d_out, down_units[-1])
    down_grads = [contract_rows(d_out[e], hiddens[e]).astype(jnp.bfloat16) for e in experts]
    down_home, down_grads, d_out = after(
        (at_home(w_down, shifts, down_units), down_grads, d_out)
    )

    leaving = back_units(units)
    down_back = [back_unit(down_grads, leaving[0], down_home)]
    d_acts, terms = [], []
    for e in experts:
        gate_act, up_act, sigmoid_gate, silu_gate, _ = acts[e]
        d_hidden = dot_f32(d_out[e], down_home[:, cut[e]], 1, 0)
        d_gate = (
            d_hidden * up_act * sigmoid_gate * (1.0 + gate_act * (1.0 - sigmoid_gate))
        ).astype(jnp.bfloat16)
        d_acts.append((d_gate, (d_hidden * silu_gate).astype(jnp.bfloat16)))
    for e in experts:
        terms.append(contract_cols(d_acts[e][0], gate_home[:, cut[e]]))
    terms, d_acts = after((terms, d_acts), down_back[0])
    for unit in leaving[1:-1]:
        down_back.append(back_unit(down_grads, unit, terms))
    d_in = [
        (terms[e] + contract_cols(d_acts[e][1], up_home[:, cut[e]])).astype(jnp.bfloat16)
        for e in experts
    ]
    d_rows = combine(slot_column, d_in, tok_rows)
    d_rows, expert_in, d_acts = after((d_rows, expert_in, d_acts), down_back)
    down_back.append(back_unit(down_grads, leaving[-1], d_rows))
    d_rows = lax.psum_scatter(d_rows, "col", scatter_dimension=1, tiled=True)
    gate_grads = [contract_rows(expert_in[e], d_acts[e][0]).astype(jnp.bfloat16) for e in experts]
    up_grads = [contract_rows(expert_in[e], d_acts[e][1]).astype(jnp.bfloat16) for e in experts]
    gate_grads, up_grads, hiddens = after((gate_grads, up_grads, hiddens), down_back[-1])
    gate_back = [back_unit(gate_grads, leaving[0])]
    gate_back.append(back_unit(gate_grads, leaving[1]))
    gated = [
        (slot_gate[e] * contract_cols(hiddens[e], down_home[:, cut[e]])).astype(jnp.bfloat16)
        for e in experts
    ]
    halves = [combine(slot_column, gated, tok_rows, half) for half in (0, 1)]
    halves = after(halves, gate_back)
    for unit in leaving[2:]:
        gate_back.append(back_unit(gate_grads, unit, halves))
    d_rows = after(d_rows, gate_back)
    d_normed_two = group_total(d_rows)
    halves[0] = lax.psum_scatter(
        after(halves[0], d_rows), "col", scatter_dimension=1, tiled=True
    )
    w_down_grad = at_owner(down_grads, leaving, down_back)
    w_gate_grad = at_owner(gate_grads, leaving, gate_back)

    gain_two = lax.dynamic_slice_in_dim(moe_norm, col_start, own_width)
    moe_dot = over_col(jnp.sum(d_normed_two * gain_two * mid_own, 1))
    d_residual = (
        cotangent.astype(jnp.float32)
        + scale_two * gain_two * d_normed_two
        - mid_own * scale_two**3 * (moe_dot / width)[:, None]
    )
    moe_gain_grad = jnp.sum(d_normed_two * mid_own * scale_two, 0)
    d_res_low = d_residual.astype(jnp.bfloat16)
    up_back = [back_unit(up_grads, unit, d_normed_two) for unit in leaving[:2]]
    d_res_low, halves[0] = after((d_res_low, halves[0]))
    d_attn_whole = after(lax.all_gather(d_res_low, "col", axis=1, tiled=True), up_back)
    halves[1] = lax.psum_scatter(
        after(halves[1], d_attn_whole), "col", scatter_dimension=1, tiled=True
    )
    moe_sums = [group_total(after(halves[0], d_attn_whole))]
    d_attended = jnp.dot(
        d_attn_whole, out_cols, preferred_element_type=jnp.float32
    ).astype(jnp.bfloat16)
    d_qn, d_kn, d_values = attend_back(
        parents, q_rot, k_rot, value_low, d_attended, cos_table, sin_table, heads
    )
    qk_dots = over_col(
        jnp.stack([jnp.sum(query * q_gain * d_qn, 1), jnp.sum(keyed * k_gain * d_kn, 1)])
    )
    qk_dots = after(qk_dots, moe_sums[0])
    for unit in leaving[2:-1]:
        up_back.append(back_unit(up_grads, unit, qk_dots))
    d_query = (
        q_scale * q_gain * d_qn - query * q_scale**3 * (qk_dots[0] / width)[:, None]
    ).astype(jnp.bfloat16)
    d_keyed = (
        k_scale * k_gain * d_kn - keyed * k_scale**3 * (qk_dots[1] / width)[:, None]
    ).astype(jnp.bfloat16)
    q_gain_grad = jnp.sum(d_qn * query * q_scale, 0)
    k_gain_grad = jnp.sum(d_kn * keyed * k_scale, 0)
    d_qkv = jnp.concatenate([d_query, d_keyed, d_values], 1)
    d_one = block_order(contract_cols(qkv_cols, d_qkv).astype(jnp.bfloat16), own_width)
    d_one = after(d_one, up_back)
    d_qkv, attended, d_attn_whole = after((d_qkv, attended, d_attn_whole), d_one)
    attn_grads = jnp.concatenate(
        [
            block_order(contract_rows(normed_one, d_qkv).astype(jnp.bfloat16), own_width),
            contract_rows(d_attn_whole, attended).astype(jnp.bfloat16),
        ],
        1,
    )
    d_one, attn_grads, halves[1] = after((d_one, attn_grads, halves[1]))
    d_normed_one = lax.psum_scatter(d_one, "col", scatter_dimension=0, tiled=True)
    attn_grads = group_total(attn_grads)
    d_normed_one = after(d_normed_one, attn_grads).astype(jnp.float32).T
    moe_sums.append(group_total(after(halves[1], attn_grads)))
    up_back.append(back_unit(up_grads, leaving[-1], moe_sums))
    w_up_grad = at_owner(up_grads, leaving, up_back)
    w_query_grad = attn_grads[:, :own_width]
    w_key_grad = attn_grads[:, own_width : 2 * own_width]
    w_value_grad = attn_grads[:, 2 * own_width : 3 * own_width]
    w_out_grad = attn_grads[:, 3 * own_width :]
    tokens_own = tokens.astype(jnp.float32)
    gain_one = lax.dynamic_slice_in_dim(attn_norm, col_start, own_width)
    attn_dot = over_col(jnp.sum(d_normed_one * gain_one * tokens_own, 1))
    tokens_grad = (
        d_residual
        + scale_one * gain_one * d_normed_one
        - tokens_own * scale_one**3 * (attn_dot / width)[:, None]
    )
    moe_sum = jnp.concatenate(moe_sums, 0)
    output = (residual + moe_sum).astype(jnp.bfloat16)
    attn_gain_grad = jnp.sum(d_normed_one * tokens_own * scale_one, 0)
    gain_grads = jnp.sum(
        row_stack(jnp.stack([attn_gain_grad, q_gain_grad, k_gain_grad, moe_gain_grad])), 0
    )
    return (
        output,
        tokens_grad,
        gain_grads[0],
        w_query_grad,
        w_key_grad,
        w_value_grad,
        gain_grads[1],
        gain_grads[2],
        w_out_grad,
        gain_grads[3],
        w_gate_grad,
        w_up_grad,
        w_down_grad,
    )


def solution(mesh):
    grid = P("row", "col")
    rows = P("row", None)
    in_specs = (
        grid,
        P(),
        grid,
        grid,
        grid,
        P(),
        P(),
        grid,
        P(),
        grid,
        grid,
        grid,
        rows,
        rows,
        rows,
        grid,
    )
    out_specs = (
        grid,
        grid,
        P("col"),
        grid,
        grid,
        grid,
        P("col"),
        P("col"),
        grid,
        P("col"),
        grid,
        grid,
        grid,
    )
    return jax.shard_map(body, mesh=mesh, in_specs=in_specs, out_specs=out_specs, check_vma=False)
```

```python
import functools
import math

import jax
import jax.numpy as jnp
from jax import lax
from jax.experimental import pallas as pl
from jax.experimental.pallas import tpu as pltpu
from jax.sharding import PartitionSpec as P

HD = 128
FF = 1024
SEG = 128
TREE = 2560
NSEG = 20
TRUNK = 512
BRANCH_END = 1024
LEAF_END = 2048
CAP = 426
CAPP = 432


EPS = 1e-05
NEGATIVE = -1e30
MIB = 1024 * 1024


def depths_of(parent_ids):
    segment_ids = jnp.arange(NSEG, dtype=jnp.int32)

    def advance(turn_index, loop_state):
        current, depth = loop_state
        matches = current[:, None] == segment_ids[None, :]
        parent_of = jnp.sum(jnp.where(matches, parent_ids[None, :], 0), 1)
        current = jnp.where(current >= 0, parent_of, -1)
        return (current, depth + (current >= 0).astype(jnp.int32))

    start = (segment_ids, jnp.zeros((NSEG,), jnp.int32))
    state = start
    for turn in range(6):
        state = advance(turn, state)
    return state[1]


def rope_tables(parent_ids):
    depths = depths_of(parent_ids)
    position = jnp.arange(TREE, dtype=jnp.int32)
    places = (jnp.repeat(depths, SEG) * SEG + position % SEG).astype(jnp.float32)
    frequency = jnp.exp(jnp.arange(HD // 2, dtype=jnp.float32) * (-2.0 * math.log(10000.0) / HD))
    angles = places[:, None] * frequency[None, :]
    cosine, sine = jnp.cos(angles), jnp.sin(angles)
    return (
        jnp.concatenate([cosine, cosine], -1),
        jnp.concatenate([-sine, sine], -1),
    )


def dot_f32(left, right, left_dim, right_dim):
    return lax.dot_general(
        left, right, (((left_dim,), (right_dim,)), ((), ())), preferred_element_type=jnp.float32
    )


def contract_rows(left, right):
    return dot_f32(left, right, 0, 0)


def contract_cols(left, right):
    return dot_f32(left, right, 1, 1)


def over_col(partial_value):
    return jnp.sum(lax.all_gather(partial_value, "col", axis=0), 0)


def after(value, *earlier):
    return lax.optimization_barrier((value,) + earlier)[0]


def gather_blocks(part):
    count = lax.axis_size("col")

    def swap(block, bits):
        return lax.ppermute(block, "col", [(i, i ^ bits) for i in range(count)])

    if count == 8:
        half = part.shape[0] // 2
        side, far, twin = swap(part, 2), swap(part, 4), swap(part, 1)
        corner = jnp.concatenate([swap(far[:half], 2), swap(side[half:], 4)], 0)
        return [
            part,
            twin,
            side,
            swap(side, 1),
            far,
            swap(far, 1),
            corner,
            swap(corner, 1),
        ]
    blocks = [part]
    bits = 1
    while bits < count:
        blocks = blocks + [swap(block, bits) for block in blocks]
        bits = bits * 2
    return blocks


def block_order(rows, depth):
    own = lax.axis_index("col")
    count = rows.shape[0] // depth
    return jnp.concatenate(
        [lax.dynamic_slice_in_dim(rows, (own ^ k) * depth, depth, 0) for k in range(count)], 0
    )


def causal(count):
    rows = lax.broadcasted_iota(jnp.int32, (count, count), 0)
    cols = lax.broadcasted_iota(jnp.int32, (count, count), 1)
    return cols <= rows


def key_starts(chunk, parent_of):
    first = chunk * 4
    blocks = [[(first + s) * SEG for s in range(4)]]
    if TRUNK * chunk >= BRANCH_END and TRUNK * chunk < LEAF_END:
        blocks.append([parent_of[first + s] * SEG for s in range(4)])
    return blocks


def seg_dot(rows, keys_ref, starts):
    return jnp.concatenate(
        [
            contract_cols(rows[s * SEG : (s + 1) * SEG], keys_ref[pl.ds(starts[s], SEG), :])
            for s in range(4)
        ],
        0,
    )


def chunk_weights(chunk, query, k_ref, blocks, scale):
    pieces = []
    if chunk == 0:
        score = contract_cols(query, k_ref[0:TRUNK, :]) * scale
        pieces.append(jnp.where(causal(TRUNK), score, NEGATIVE))
    else:
        if TRUNK * chunk < LEAF_END:
            pieces.append(contract_cols(query, k_ref[0:TRUNK, :]) * scale)
        mask = jnp.concatenate([causal(SEG)] * 4, 0)
        pieces.append(jnp.where(mask, seg_dot(query, k_ref, blocks[0]) * scale, NEGATIVE))
        for starts in blocks[1:]:
            pieces.append(seg_dot(query, k_ref, starts) * scale)
    highest = jnp.max(pieces[0], -1, keepdims=True)
    for piece in pieces[1:]:
        highest = jnp.maximum(highest, jnp.max(piece, -1, keepdims=True))
    raised = [jnp.exp(piece - highest) for piece in pieces]
    total = jnp.sum(raised[0], -1, keepdims=True)
    for piece in raised[1:]:
        total = total + jnp.sum(piece, -1, keepdims=True)
    inverse = 1.0 / total
    return [piece * inverse for piece in raised]


def chunk_parts(chunk, pieces, blocks):
    places = []
    if chunk == 0:
        places = [None]
    else:
        if TRUNK * chunk < LEAF_END:
            places.append(None)
        places = places + blocks
    return list(zip(pieces, places))


def forward_kernel(
    parents_ref,
    q_ref,
    k_ref,
    v_ref,
    qs_ref,
    ks_ref,
    qg_ref,
    kg_ref,
    cos_ref,
    sin_ref,
    att_ref,
    qr_ref,
    kr_ref,
    vl_ref,
):
    tree = pl.program_id(0)
    scale = 1.0 / math.sqrt(HD)
    parent_of = [parents_ref[tree, s] for s in range(NSEG)]

    def turned(field):
        return field * cos_ref[...] + pltpu.roll(field, HD // 2, 1) * sin_ref[...]

    qr_ref[...] = turned(q_ref[...] * qs_ref[...] * qg_ref[...]).astype(jnp.bfloat16)
    kr_ref[...] = turned(k_ref[...] * ks_ref[...] * kg_ref[...]).astype(jnp.bfloat16)
    vl_ref[...] = v_ref[...].astype(jnp.bfloat16)
    for chunk in range(TREE // TRUNK):
        rows = slice(chunk * TRUNK, (chunk + 1) * TRUNK)
        blocks = key_starts(chunk, parent_of)
        weights = chunk_weights(chunk, qr_ref[rows, :], kr_ref, blocks, scale)
        total = jnp.zeros((TRUNK, HD), jnp.float32)
        for weight, starts in chunk_parts(chunk, weights, blocks):
            low = weight.astype(jnp.bfloat16)
            if starts is None:
                total = total + dot_f32(low, vl_ref[0:TRUNK, :], 1, 0)
            else:
                total = total + jnp.concatenate(
                    [
                        dot_f32(
                            low[s * SEG : (s + 1) * SEG], vl_ref[pl.ds(starts[s], SEG), :], 1, 0
                        )
                        for s in range(4)
                    ],
                    0,
                )
        att_ref[rows, :] = total.astype(jnp.bfloat16)


def backward_kernel(
    parents_ref,
    qr_ref,
    kr_ref,
    vl_ref,
    do_ref,
    cos_ref,
    sin_ref,
    dq_ref,
    dk_ref,
    dv_ref,
    dv_acc,
):
    tree = pl.program_id(0)
    scale = 1.0 / math.sqrt(HD)
    parent_of = [parents_ref[tree, s] for s in range(NSEG)]
    dk_ref[...] = jnp.zeros_like(dk_ref)
    dv_acc[...] = jnp.zeros_like(dv_acc)
    for chunk in range(TREE // TRUNK):
        rows = slice(chunk * TRUNK, (chunk + 1) * TRUNK)
        blocks = key_starts(chunk, parent_of)
        query = qr_ref[rows, :]
        grad = do_ref[rows, :]
        weights = chunk_weights(chunk, query, kr_ref, blocks, scale)
        parts = chunk_parts(chunk, weights, blocks)
        d_weights = []
        row_dot = jnp.zeros((TRUNK, 1), jnp.float32)
        for weight, starts in parts:
            if starts is None:
                d_weight = contract_cols(grad, vl_ref[0:TRUNK, :])
            else:
                d_weight = seg_dot(grad, vl_ref, starts)
            d_weights.append(d_weight)
            row_dot = row_dot + jnp.sum(weight * d_weight, -1, keepdims=True)
        d_query = jnp.zeros((TRUNK, HD), jnp.float32)
        for (weight, starts), d_weight in zip(parts, d_weights):
            low = weight.astype(jnp.bfloat16)
            d_score = (weight * (d_weight - row_dot)).astype(jnp.bfloat16)
            if starts is None:
                d_query = d_query + dot_f32(d_score, kr_ref[0:TRUNK, :], 1, 0)
                dk_ref[0:TRUNK, :] += contract_rows(d_score, query)
                dv_acc[0:TRUNK, :] += contract_rows(low, grad)
            else:
                turns = []
                for s in range(4):
                    own = slice(s * SEG, (s + 1) * SEG)
                    keys = pl.ds(starts[s], SEG)
                    turns.append(dot_f32(d_score[own], kr_ref[keys, :], 1, 0))
                    dk_ref[keys, :] += contract_rows(d_score[own], query[own])
                    dv_acc[keys, :] += contract_rows(low[own], grad[own])
                d_query = d_query + jnp.concatenate(turns, 0)
        dq_ref[rows, :] = d_query

    def unturned(field):
        return (field * cos_ref[...] - pltpu.roll(field, HD // 2, 1) * sin_ref[...]) * scale

    dq_ref[...] = unturned(dq_ref[...])
    dk_ref[...] = unturned(dk_ref[...])
    dv_ref[...] = dv_acc[...].astype(jnp.bfloat16)


def attend(parents, qkv, q_scale, k_scale, q_gain, k_gain, cos_table, sin_table, heads):
    trees = parents.shape[0]
    rows = qkv.shape[0]

    def field(shift):
        return pl.BlockSpec((TREE, HD), lambda t, h, p: (t, h + shift))

    scale_spec = pl.BlockSpec((TREE, 1), lambda t, h, p: (t, 0))
    gain_spec = pl.BlockSpec((1, HD), lambda t, h, p: (0, h))
    table = pl.BlockSpec((TREE, HD), lambda t, h, p: (t, 0))
    return pl.pallas_call(
        forward_kernel,
        grid_spec=pltpu.PrefetchScalarGridSpec(
            num_scalar_prefetch=1,
            grid=(trees, heads),
            in_specs=[
                field(0),
                field(heads),
                field(2 * heads),
                scale_spec,
                scale_spec,
                gain_spec,
                gain_spec,
                table,
                table,
            ],
            out_specs=[field(0)] * 4,
        ),
        out_shape=[jax.ShapeDtypeStruct((rows, heads * HD), jnp.bfloat16)] * 4,
        compiler_params=pltpu.CompilerParams(vmem_limit_bytes=50 * MIB),
        name="tree_forward",
    )(
        parents,
        qkv,
        qkv,
        qkv,
        q_scale,
        k_scale,
        q_gain[None, :],
        k_gain[None, :],
        cos_table,
        sin_table,
    )


def attend_back(parents, q_rot, k_rot, values, d_attended, cos_table, sin_table, heads):
    trees = parents.shape[0]
    rows = q_rot.shape[0]
    field = pl.BlockSpec((TREE, HD), lambda t, h, p: (t, h))
    table = pl.BlockSpec((TREE, HD), lambda t, h, p: (t, 0))
    return pl.pallas_call(
        backward_kernel,
        grid_spec=pltpu.PrefetchScalarGridSpec(
            num_scalar_prefetch=1,
            grid=(trees, heads),
            in_specs=[field, field, field, field, table, table],
            out_specs=[field] * 3,
            scratch_shapes=[pltpu.VMEM((TREE, HD), jnp.float32)],
        ),
        out_shape=[
            jax.ShapeDtypeStruct((rows, heads * HD), jnp.float32),
            jax.ShapeDtypeStruct((rows, heads * HD), jnp.float32),
            jax.ShapeDtypeStruct((rows, heads * HD), jnp.bfloat16),
        ],
        compiler_params=pltpu.CompilerParams(vmem_limit_bytes=50 * MIB),
        name="tree_backward",
    )(parents, q_rot, k_rot, values, d_attended, cos_table, sin_table)


def slots_kernel(slot_ref, gate_ref, gain_ref, x_ref, *refs, normed):
    units = slot_ref.shape[1]
    outs, gate_out, acc, gate_acc = refs[:units], refs[units], refs[units + 1], refs[units + 2]
    step = pl.program_id(1)

    @pl.when(step == 0)
    def _():
        acc[...] = jnp.zeros_like(acc)
        gate_acc[...] = jnp.zeros_like(gate_acc)

    for e in range(units):
        slots = lax.broadcasted_iota(jnp.int32, (CAPP, x_ref.shape[0]), 0)
        picks = slot_ref[0, e : e + 1, :] == slots
        acc[e] += dot_f32(picks.astype(jnp.bfloat16), x_ref[...], 1, 0)
        gate_acc[e] += jnp.sum(jnp.where(picks, gate_ref[0, e : e + 1, :], 0.0), 1, keepdims=True)

    @pl.when(step == pl.num_programs(1) - 1)
    def _():
        for e in range(units):
            rows = acc[e]
            if normed:
                scale = lax.rsqrt(jnp.mean(rows * rows, 1, keepdims=True) + EPS)
                outs[e][...] = (rows * scale * gain_ref[...]).astype(jnp.bfloat16)
            else:
                outs[e][...] = (gate_acc[e] * rows).astype(jnp.bfloat16)
            gate_out[e] = gate_acc[e]


def to_slots(slot_of, token_gate, gain, rows, normed):
    groups, units, tok_rows = slot_of.shape
    width = rows.shape[1]
    block = tok_rows // 2
    steps = tok_rows // block
    table = pl.BlockSpec((1, units, block), lambda g, t: (g, 0, t))
    out = pl.pallas_call(
        functools.partial(slots_kernel, normed=normed),
        grid=(groups, steps),
        in_specs=[
            table,
            table,
            pl.BlockSpec((1, width), lambda g, t: (0, 0)),
            pl.BlockSpec((block, width), lambda g, t: (g * steps + t, 0)),
        ],
        out_specs=[pl.BlockSpec((CAPP, width), lambda g, t: (g, 0))] * units
        + [pl.BlockSpec((units, CAPP, 1), lambda g, t: (0, g, 0))],
        out_shape=[jax.ShapeDtypeStruct((groups * CAPP, width), jnp.bfloat16)] * units
        + [jax.ShapeDtypeStruct((units, groups * CAPP, 1), jnp.float32)],
        scratch_shapes=[
            pltpu.VMEM((units, CAPP, width), jnp.float32),
            pltpu.VMEM((units, CAPP, 1), jnp.float32),
        ],
        compiler_params=pltpu.CompilerParams(vmem_limit_bytes=56 * MIB),
        cost_estimate=pl.CostEstimate(
            flops=2 * groups * tok_rows * units * CAPP * width,
            bytes_accessed=2 * groups * tok_rows * width,
            transcendentals=0,
        ),
        name="slots",
    )(slot_of, token_gate, gain[None, :], rows)
    return out[:units], out[units]


def combine_kernel(slot_ref, *refs):
    out_ref = refs[-1]
    total = None
    for e, y_ref in enumerate(refs[:-1]):
        slots = lax.broadcasted_iota(jnp.int32, (slot_ref.shape[0], CAPP), 1)
        picks = (slot_ref[:, e : e + 1] == slots).astype(jnp.bfloat16)
        term = dot_f32(picks, y_ref[0], 1, 0)
        total = term if total is None else total + term
    out_ref[...] = total.astype(out_ref.dtype)


def combine(slot_of, slot_rows, tok_rows, half=None):
    units, width = len(slot_rows), slot_rows[0].shape[1]
    groups = slot_rows[0].shape[0] // CAPP
    block = tok_rows // 4
    steps = 4 if half is None else 2
    first = 0 if half is None else 2 * half
    rows_spec = pl.BlockSpec((1, CAPP, width), lambda g, t: (g, 0, 0))
    return pl.pallas_call(
        combine_kernel,
        grid=(groups, steps),
        in_specs=[pl.BlockSpec((block, units), lambda g, t: (g * 4 + first + t, 0))]
        + [rows_spec] * units,
        out_specs=pl.BlockSpec((block, width), lambda g, t: (g * steps + t, 0)),
        out_shape=jax.ShapeDtypeStruct((groups * steps * block, width), jnp.bfloat16),
        compiler_params=pltpu.CompilerParams(vmem_limit_bytes=50 * MIB),
        cost_estimate=pl.CostEstimate(
            flops=2 * groups * steps * block * units * CAPP * width,
            bytes_accessed=2 * groups * steps * block * width,
            transcendentals=0,
        ),
        name="combine",
    )(slot_of, *[rows.reshape(groups, CAPP, width) for rows in slot_rows])


def shift_row(block, k):
    count = lax.axis_size("row")
    return lax.ppermute(block, "row", [(i, (i + k) % count) for i in range(count)])


def row_stack(part, *earlier):
    count = lax.axis_size("row")
    here = lax.axis_index("row")
    part = after(part, *earlier)
    whole = jnp.zeros((count,) + part.shape, part.dtype)
    for k in range(count):
        block = part if k == 0 else shift_row(part, k)
        whole = lax.dynamic_update_slice_in_dim(whole, block[None], (here - k) % count, 0)
    return whole


def crossing_units():
    count = lax.axis_size("row")
    units = []
    for k in range(1, count):
        parts = 1 if k in (1, count - 1) else 2
        units = units + [(k, part, parts) for part in range(parts)]
    return units


def home_unit(weight, unit, *earlier):
    k, part, parts = unit
    groups = lax.axis_size("row")
    share = weight.shape[1] // groups
    to = (lax.axis_index("row") + k) % groups
    block = lax.dynamic_slice_in_dim(
        after(weight, *earlier), to * share + part * (share // parts), share // parts, 1
    )
    return shift_row(block, k)


def home_kernel(here_ref, own_ref, *refs, units, groups):
    out_ref = refs[-1]
    source = lax.rem(here_ref[0] - pl.program_id(0) + groups, groups)

    @pl.when(source == 0)
    def _():
        out_ref[...] = own_ref[...]

    for (k, part, parts), block_ref in zip(units, refs[:-1]):
        wide = out_ref.shape[1] // parts

        @pl.when(source == k)
        def _(block_ref=block_ref, start=part * wide, wide=wide):
            out_ref[:, start : start + wide] = block_ref[...]


def at_home(weight, units, blocks):
    groups = lax.axis_size("row")
    depth, columns = weight.shape
    share = columns // groups
    return pl.pallas_call(
        functools.partial(home_kernel, units=units, groups=groups),
        grid_spec=pltpu.PrefetchScalarGridSpec(
            num_scalar_prefetch=1,
            grid=(groups,),
            in_specs=[pl.BlockSpec((depth, share), lambda j, here: (0, here[0]))]
            + [pl.BlockSpec(block.shape, lambda j, here: (0, 0)) for block in blocks],
            out_specs=pl.BlockSpec((depth, share), lambda j, here: (j, 0)),
        ),
        out_shape=jax.ShapeDtypeStruct((depth * groups, share), weight.dtype),
        compiler_params=pltpu.CompilerParams(vmem_limit_bytes=50 * MIB),
        cost_estimate=pl.CostEstimate(
            flops=0, bytes_accessed=4 * depth * columns, transcendentals=0
        ),
        name="at_home",
    )(lax.axis_index("row").astype(jnp.int32)[None], weight, *blocks)


def back_units(count):
    rows = lax.axis_size("row")
    units = []
    for k in range(1, rows):
        if k in (1, rows - 1):
            units.append((k, tuple(range(count))))
        else:
            units = units + [(k, (e,)) for e in range(count)]
    return units


def back_unit(grads, unit, *earlier):
    k, which = unit
    groups = lax.axis_size("row")
    depth = grads[0].shape[0] // groups
    to = (lax.axis_index("row") + k) % groups
    chosen = after([grads[e] for e in which], *earlier)
    return [
        shift_row(lax.dynamic_slice_in_dim(grad, to * depth, depth, 0), k) for grad in chosen
    ]


def owner_kernel(here_ref, *refs, units, groups, count):
    out_ref = refs[-1]
    hidden = refs[0].shape[1]
    source = lax.rem(here_ref[0] - pl.program_id(0) + groups, groups)
    places = [(0, e) for e in range(count)]
    places = places + [(k, e) for k, which in units for e in which]
    for (k, e), block_ref in zip(places, refs[:-1]):

        @pl.when(source == k)
        def _(block_ref=block_ref, start=e * hidden):
            out_ref[:, start : start + hidden] = block_ref[...].astype(jnp.float32)


def at_owner(grads, units, received):
    groups = lax.axis_size("row")
    depth, hidden = grads[0].shape[0] // groups, grads[0].shape[1]
    count = len(grads)
    share = hidden * count
    blocks = [block for pair in received for block in pair]
    return pl.pallas_call(
        functools.partial(owner_kernel, units=units, groups=groups, count=count),
        grid_spec=pltpu.PrefetchScalarGridSpec(
            num_scalar_prefetch=1,
            grid=(groups,),
            in_specs=[pl.BlockSpec((depth, hidden), lambda j, here: (here[0], 0))] * count
            + [pl.BlockSpec((depth, hidden), lambda j, here: (0, 0))] * len(blocks),
            out_specs=pl.BlockSpec((depth, share), lambda j, here: (0, j)),
        ),
        out_shape=jax.ShapeDtypeStruct((depth, share * groups), jnp.float32),
        compiler_params=pltpu.CompilerParams(vmem_limit_bytes=50 * MIB),
        cost_estimate=pl.CostEstimate(
            flops=0, bytes_accessed=6 * depth * share * groups, transcendentals=0
        ),
        name="at_owner",
    )(lax.axis_index("row").astype(jnp.int32)[None], *grads, *blocks)


def line_steps(part, *earlier):
    count = lax.axis_size("row")
    upward = downward = part
    steps = []
    for _ in range(count - 1):
        upward, downward = after((upward, downward), *earlier)
        upward = lax.ppermute(upward, "row", [(i, i + 1) for i in range(count - 1)])
        downward = lax.ppermute(downward, "row", [(i + 1, i) for i in range(count - 1)])
        earlier = (upward, downward)
        steps.append((upward, downward))
    return steps


def line_gather(part, steps):
    count = lax.axis_size("row")
    here = lax.axis_index("row")
    rows = part.shape[0]
    whole = jnp.zeros((rows * count, part.shape[1]), part.dtype)
    whole = lax.dynamic_update_slice_in_dim(whole, part, here * rows, 0)
    for k in range(1, count):
        block = jnp.where(here >= k, steps[k - 1][0], steps[count - k - 1][1])
        whole = lax.dynamic_update_slice_in_dim(whole, block, ((here - k) % count) * rows, 0)
    return whole


def group_total(part, along=()):
    groups = lax.axis_size("row")
    here = lax.axis_index("row")
    rows = part.shape[0] // groups

    def rows_of(group):
        start = jnp.clip(group, 0, groups - 1) * rows
        return lax.dynamic_slice_in_dim(part, start, rows, 0).astype(jnp.float32)

    upward = downward = 0.0
    for step in range(1, groups):
        upward = (rows_of(here + groups - step) + upward).astype(jnp.bfloat16)
        downward = (rows_of(here - groups + step) + downward).astype(jnp.bfloat16)
        upward = lax.ppermute(upward, "row", [(i, i + 1) for i in range(step)])
        downward = lax.ppermute(downward, "row", [(groups - 1 - i, groups - 2 - i) for i in range(step)])
        upward, downward = after((upward, downward), *(along if step == groups - 2 else ()))
        upward, downward = upward.astype(jnp.float32), downward.astype(jnp.float32)
    return rows_of(here) + upward + downward


def body(
    tokens,
    attn_norm,
    w_query,
    w_key,
    w_value,
    q_norm,
    k_norm,
    w_out,
    moe_norm,
    w_gate,
    w_up,
    w_down,
    routes,
    gates,
    parents,
    cotangent,
):
    tok_rows, own_width = tokens.shape
    groups = lax.axis_size("row")
    cols = lax.axis_size("col")
    width = own_width * cols
    here, col = lax.axis_index("row"), lax.axis_index("col")
    col_start = col * own_width
    heads = own_width // HD
    trees = parents.shape[0]

    qkv_cols = lax.all_gather(
        jnp.concatenate([w_query, w_key, w_value], 1), "row", axis=0, tiled=True
    )
    out_cols = lax.all_gather(after(w_out, qkv_cols), "row", axis=0, tiled=True)
    shifts = crossing_units()
    last = len(shifts) - 1
    grad_steps = line_steps(cotangent, qkv_cols)

    wide = jnp.concatenate(gather_blocks(tokens), 1).astype(jnp.float32)
    cos_table, sin_table = jax.vmap(rope_tables)(parents)
    cos_table, sin_table = cos_table.reshape(-1, HD), sin_table.reshape(-1, HD)
    scale_one = lax.rsqrt(jnp.mean(wide * wide, 1, keepdims=True) + EPS)
    norm_gain = block_order(attn_norm, own_width)
    normed_one = (wide * scale_one * norm_gain[None, :]).astype(jnp.bfloat16)
    qkv_cols = block_order(qkv_cols, own_width)
    qkv = jnp.dot(normed_one, qkv_cols, preferred_element_type=jnp.float32)
    query, keyed = qkv[:, :own_width], qkv[:, own_width : 2 * own_width]
    squares = over_col(jnp.stack([jnp.sum(query * query, 1), jnp.sum(keyed * keyed, 1)]))
    q_scale = lax.rsqrt(squares[0] / width + EPS)[:, None]
    k_scale = lax.rsqrt(squares[1] / width + EPS)[:, None]
    q_gain = lax.dynamic_slice_in_dim(q_norm, col_start, own_width)
    k_gain = lax.dynamic_slice_in_dim(k_norm, col_start, own_width)
    q_scale = after(q_scale, grad_steps[0])
    attended, q_rot, k_rot, value_low = attend(
        parents, qkv, q_scale, k_scale, q_gain, k_gain, cos_table, sin_table, heads
    )
    attn_sum = lax.psum_scatter(
        after(contract_cols(attended, out_cols).astype(jnp.bfloat16), grad_steps[:-1]),
        "col",
        scatter_dimension=1,
        tiled=True,
    )
    route_all = row_stack(routes.T, grad_steps[:-1])
    gate_all = row_stack(gates.T, grad_steps[:-1])
    gate_units = [home_unit(w_gate, shifts[0], grad_steps[:-1])]
    attn_sum = after(attn_sum, gate_units, grad_steps, route_all, gate_all)
    residual = tokens.astype(jnp.float32) + attn_sum.astype(jnp.float32)
    mid_low = residual.astype(jnp.bfloat16)
    mid_own = mid_low.astype(jnp.float32)
    mid_row = lax.all_gather(mid_low, "row", axis=0, tiled=True)
    gate_units.append(home_unit(w_gate, shifts[1], mid_low))
    grad_row = line_gather(cotangent, grad_steps)

    share = w_gate.shape[1] // groups
    units, hidden_units = max(1, share // FF), min(share, FF)
    first_unit = col * (w_gate.shape[1] // FF) + (here * share) // FF
    unit_ids = first_unit + jnp.arange(units, dtype=jnp.int32)
    match = route_all[None] == unit_ids[:, None, None, None]
    named = jnp.any(match, 2)
    token_gate = jnp.sum(jnp.where(match, gate_all[None], 0.0), 2)
    rank = jnp.cumsum(named.astype(jnp.int32), 2) - 1
    slot_of = jnp.where(named, rank, -1)
    slot_of, token_gate = slot_of.transpose(1, 0, 2), token_gate.transpose(1, 0, 2)
    slot_column = slot_of.transpose(0, 2, 1).reshape(groups * tok_rows, units)
    mid_row, slot_of, token_gate, slot_column, grad_row = after(
        (mid_row, slot_of, token_gate, slot_column, grad_row), gate_units
    )
    mid_all = lax.all_gather(mid_row, "col", axis=1, tiled=True)
    scale_two = lax.rsqrt(over_col(jnp.sum(mid_own * mid_own, 1)) / width + EPS)[:, None]
    for unit in shifts[2:]:
        gate_units.append(home_unit(w_gate, unit, gate_units[-1], mid_row))
    gate_home = at_home(w_gate, shifts, gate_units)
    up_units = [home_unit(w_up, shifts[0], gate_units[-1])]
    for unit in shifts[1:last]:
        up_units.append(home_unit(w_up, unit, up_units[-1]))
    mid_all, gate_home = after((mid_all, gate_home), up_units[-2])
    grad_all = lax.all_gather(after(grad_row, mid_all), "col", axis=1, tiled=True)

    experts = range(units)
    cut = [slice(e * hidden_units, (e + 1) * hidden_units) for e in experts]
    expert_in, slot_gate = to_slots(slot_of, token_gate, moe_norm, mid_all, True)
    expert_in = after(expert_in, up_units[-1])
    up_units = after(up_units, expert_in)
    up_units.append(home_unit(w_up, shifts[last], up_units[-1], expert_in))
    gate_acts = [dot_f32(expert_in[e], gate_home[:, cut[e]], 1, 0) for e in experts]
    up_home, gate_acts = after((at_home(w_up, shifts, up_units), gate_acts))
    down_units = [home_unit(w_down, shifts[0], up_home)]
    acts = []
    for e in experts:
        up_act = dot_f32(expert_in[e], up_home[:, cut[e]], 1, 0)
        sigmoid_gate = jax.nn.sigmoid(gate_acts[e])
        silu_gate = gate_acts[e] * sigmoid_gate
        hidden = (silu_gate * up_act).astype(jnp.bfloat16)
        acts.append((gate_acts[e], up_act, sigmoid_gate, silu_gate, hidden))
    hiddens = after([act[-1] for act in acts], down_units[0])
    down_units.append(home_unit(w_down, shifts[1], hiddens))
    grad_all = after(grad_all, down_units[1])
    for unit in shifts[2:last]:
        down_units.append(home_unit(w_down, unit, grad_all))
    d_out, _ = to_slots(slot_of, token_gate, moe_norm, grad_all, False)
    d_out = after(d_out, down_units[-1])
    down_units.append(home_unit(w_down, shifts[last], d_out))
    down_grads = [contract_rows(d_out[e], hiddens[e]).astype(jnp.bfloat16) for e in experts]
    down_grads, d_out, down_units = after((down_grads, d_out, down_units))
    down_home = at_home(w_down, shifts, down_units)

    leaving = back_units(units)
    down_back = [back_unit(down_grads, leaving[0])]
    d_acts, terms = [], []
    for e in experts:
        gate_act, up_act, sigmoid_gate, silu_gate, _ = acts[e]
        d_hidden = dot_f32(d_out[e], down_home[:, cut[e]], 1, 0)
        d_gate = (
            d_hidden * up_act * sigmoid_gate * (1.0 + gate_act * (1.0 - sigmoid_gate))
        ).astype(jnp.bfloat16)
        d_acts.append((d_gate, (d_hidden * silu_gate).astype(jnp.bfloat16)))
    for e in experts:
        terms.append(contract_cols(d_acts[e][0], gate_home[:, cut[e]]))
    terms, d_acts = after((terms, d_acts), down_back[0])
    for unit in leaving[1:-1]:
        down_back.append(back_unit(down_grads, unit, terms))
    d_in = [
        (terms[e] + contract_cols(d_acts[e][1], up_home[:, cut[e]])).astype(jnp.bfloat16)
        for e in experts
    ]
    d_rows = combine(slot_column, d_in, tok_rows)
    d_rows, expert_in, d_acts = after((d_rows, expert_in, d_acts), down_back)
    down_back.append(back_unit(down_grads, leaving[-1], d_rows))
    d_rows = lax.psum_scatter(d_rows, "col", scatter_dimension=1, tiled=True)
    gate_grads = [contract_rows(expert_in[e], d_acts[e][0]).astype(jnp.bfloat16) for e in experts]
    up_grads = [contract_rows(expert_in[e], d_acts[e][1]).astype(jnp.bfloat16) for e in experts]
    gate_grads, up_grads, hiddens = after((gate_grads, up_grads, hiddens), down_back[-1])
    gate_back = [back_unit(gate_grads, leaving[0])]
    gate_back.append(back_unit(gate_grads, leaving[1]))
    gated = [
        (slot_gate[e] * contract_cols(hiddens[e], down_home[:, cut[e]])).astype(jnp.bfloat16)
        for e in experts
    ]
    halves = [combine(slot_column, gated, tok_rows, half) for half in (0, 1)]
    halves = after(halves, gate_back)
    for unit in leaving[2:]:
        gate_back.append(back_unit(gate_grads, unit, halves))
    d_rows = after(d_rows, gate_back)
    up_back = [back_unit(up_grads, leaving[0], d_rows)]
    d_normed_two = group_total(d_rows, up_back[0])
    halves[0] = lax.psum_scatter(
        after(halves[0], d_rows), "col", scatter_dimension=1, tiled=True
    )
    w_down_grad = at_owner(down_grads, leaving, down_back)
    w_gate_grad = at_owner(gate_grads, leaving, gate_back)

    gain_two = lax.dynamic_slice_in_dim(moe_norm, col_start, own_width)
    moe_dot = over_col(jnp.sum(d_normed_two * gain_two * mid_own, 1))
    d_residual = (
        cotangent.astype(jnp.float32)
        + scale_two * gain_two * d_normed_two
        - mid_own * scale_two**3 * (moe_dot / width)[:, None]
    )
    moe_gain_grad = jnp.sum(d_normed_two * mid_own * scale_two, 0)
    d_res_low = d_residual.astype(jnp.bfloat16)
    up_back.append(back_unit(up_grads, leaving[1], d_normed_two))
    d_res_low, halves[0], w_down_grad = after((d_res_low, halves[0], w_down_grad))
    d_attn_whole = lax.all_gather(d_res_low, "col", axis=1, tiled=True)
    d_attn_whole, w_gate_grad = after((d_attn_whole, w_gate_grad), up_back)
    halves[1] = lax.psum_scatter(
        after(halves[1], d_attn_whole), "col", scatter_dimension=1, tiled=True
    )
    moe_sums = [group_total(after(halves[0], d_attn_whole))]
    d_attended = jnp.dot(
        d_attn_whole, out_cols, preferred_element_type=jnp.float32
    ).astype(jnp.bfloat16)
    d_qn, d_kn, d_values = attend_back(
        parents, q_rot, k_rot, value_low, d_attended, cos_table, sin_table, heads
    )
    qk_dots = over_col(
        jnp.stack([jnp.sum(query * q_gain * d_qn, 1), jnp.sum(keyed * k_gain * d_kn, 1)])
    )
    up_back.append(back_unit(up_grads, leaving[2], d_attn_whole))
    qk_dots = after(qk_dots, moe_sums[0], up_back)
    for unit in leaving[3:]:
        up_back.append(back_unit(up_grads, unit, up_back[2], qk_dots))
    d_query = (
        q_scale * q_gain * d_qn - query * q_scale**3 * (qk_dots[0] / width)[:, None]
    ).astype(jnp.bfloat16)
    d_keyed = (
        k_scale * k_gain * d_kn - keyed * k_scale**3 * (qk_dots[1] / width)[:, None]
    ).astype(jnp.bfloat16)
    q_gain_grad = jnp.sum(d_qn * query * q_scale, 0)
    k_gain_grad = jnp.sum(d_kn * keyed * k_scale, 0)
    d_qkv = jnp.concatenate([d_query, d_keyed, d_values], 1)
    d_one = block_order(contract_cols(qkv_cols, d_qkv).astype(jnp.bfloat16), own_width)
    d_qkv, attended, d_attn_whole = after((d_qkv, attended, d_attn_whole), d_one)
    attn_grads = jnp.concatenate(
        [
            block_order(contract_rows(normed_one, d_qkv).astype(jnp.bfloat16), own_width),
            contract_rows(d_attn_whole, attended).astype(jnp.bfloat16),
        ],
        1,
    )
    d_one, attn_grads, halves[1] = after((d_one, attn_grads, halves[1]), up_back[-1])
    w_up_grad = at_owner(up_grads, leaving, up_back)
    d_normed_one = lax.psum_scatter(d_one, "col", scatter_dimension=0, tiled=True)
    attn_grads = group_total(attn_grads)
    moe_sums.append(group_total(halves[1]))
    d_normed_one, w_up_grad = after((d_normed_one, w_up_grad))
    d_normed_one = d_normed_one.astype(jnp.float32).T
    w_query_grad = attn_grads[:, :own_width]
    w_key_grad = attn_grads[:, own_width : 2 * own_width]
    w_value_grad = attn_grads[:, 2 * own_width : 3 * own_width]
    w_out_grad = attn_grads[:, 3 * own_width :]
    tokens_own = tokens.astype(jnp.float32)
    gain_one = lax.dynamic_slice_in_dim(attn_norm, col_start, own_width)
    attn_dot = over_col(jnp.sum(d_normed_one * gain_one * tokens_own, 1))
    tokens_grad = (
        d_residual
        + scale_one * gain_one * d_normed_one
        - tokens_own * scale_one**3 * (attn_dot / width)[:, None]
    )
    attn_gain_grad = jnp.sum(d_normed_one * tokens_own * scale_one, 0)
    gain_grads = jnp.sum(
        row_stack(jnp.stack([attn_gain_grad, q_gain_grad, k_gain_grad, moe_gain_grad])), 0
    )
    moe_sum = after(jnp.concatenate(moe_sums, 0), gain_grads)
    output = (residual + moe_sum).astype(jnp.bfloat16)
    return (
        output,
        tokens_grad,
        gain_grads[0],
        w_query_grad,
        w_key_grad,
        w_value_grad,
        gain_grads[1],
        gain_grads[2],
        w_out_grad,
        gain_grads[3],
        w_gate_grad,
        w_up_grad,
        w_down_grad,
    )


def solution(mesh):
    grid = P("row", "col")
    rows = P("row", None)
    in_specs = (
        grid,
        P(),
        grid,
        grid,
        grid,
        P(),
        P(),
        grid,
        P(),
        grid,
        grid,
        grid,
        rows,
        rows,
        rows,
        grid,
    )
    out_specs = (
        grid,
        grid,
        P("col"),
        grid,
        grid,
        grid,
        P("col"),
        P("col"),
        grid,
        P("col"),
        grid,
        grid,
        grid,
    )
    return jax.shard_map(body, mesh=mesh, in_specs=in_specs, out_specs=out_specs, check_vma=False)
```

```python
import functools
import math

import jax
import jax.numpy as jnp
from jax import lax
from jax.experimental import pallas as pl
from jax.experimental.pallas import tpu as pltpu
from jax.sharding import PartitionSpec as P

HD = 128
FF = 1024
SEG = 128
TREE = 2560
NSEG = 20
TRUNK = 512
BRANCH_END = 1024
LEAF_END = 2048
CAP = 426
CAPP = 432


EPS = 1e-05
NEGATIVE = -1e30
MIB = 1024 * 1024


def depths_of(parent_ids):
    segment_ids = jnp.arange(NSEG, dtype=jnp.int32)

    def advance(turn_index, loop_state):
        current, depth = loop_state
        matches = current[:, None] == segment_ids[None, :]
        parent_of = jnp.sum(jnp.where(matches, parent_ids[None, :], 0), 1)
        current = jnp.where(current >= 0, parent_of, -1)
        return (current, depth + (current >= 0).astype(jnp.int32))

    start = (segment_ids, jnp.zeros((NSEG,), jnp.int32))
    state = start
    for turn in range(6):
        state = advance(turn, state)
    return state[1]


def rope_tables(parent_ids):
    depths = depths_of(parent_ids)
    position = jnp.arange(TREE, dtype=jnp.int32)
    places = (jnp.repeat(depths, SEG) * SEG + position % SEG).astype(jnp.float32)
    frequency = jnp.exp(jnp.arange(HD // 2, dtype=jnp.float32) * (-2.0 * math.log(10000.0) / HD))
    angles = places[:, None] * frequency[None, :]
    cosine, sine = jnp.cos(angles), jnp.sin(angles)
    return (
        jnp.concatenate([cosine, cosine], -1),
        jnp.concatenate([-sine, sine], -1),
    )


def dot_f32(left, right, left_dim, right_dim):
    return lax.dot_general(
        left, right, (((left_dim,), (right_dim,)), ((), ())), preferred_element_type=jnp.float32
    )


def contract_rows(left, right):
    return dot_f32(left, right, 0, 0)


def contract_cols(left, right):
    return dot_f32(left, right, 1, 1)


def over_col(partial_value):
    return jnp.sum(lax.all_gather(partial_value, "col", axis=0), 0)


def after(value, *earlier):
    return lax.optimization_barrier((value,) + earlier)[0]


def gather_blocks(part):
    count = lax.axis_size("col")

    def swap(block, bits):
        return lax.ppermute(block, "col", [(i, i ^ bits) for i in range(count)])

    if count == 8:
        half = part.shape[0] // 2
        side, far, twin = swap(part, 2), swap(part, 4), swap(part, 1)
        corner = jnp.concatenate([swap(far[:half], 2), swap(side[half:], 4)], 0)
        return [
            part,
            twin,
            side,
            swap(side, 1),
            far,
            swap(far, 1),
            corner,
            swap(corner, 1),
        ]
    blocks = [part]
    bits = 1
    while bits < count:
        blocks = blocks + [swap(block, bits) for block in blocks]
        bits = bits * 2
    return blocks


def block_order(rows, depth):
    own = lax.axis_index("col")
    count = rows.shape[0] // depth
    return jnp.concatenate(
        [lax.dynamic_slice_in_dim(rows, (own ^ k) * depth, depth, 0) for k in range(count)], 0
    )


def causal(count):
    rows = lax.broadcasted_iota(jnp.int32, (count, count), 0)
    cols = lax.broadcasted_iota(jnp.int32, (count, count), 1)
    return cols <= rows


def key_starts(chunk, parent_of):
    first = chunk * 4
    blocks = [[(first + s) * SEG for s in range(4)]]
    if TRUNK * chunk >= BRANCH_END and TRUNK * chunk < LEAF_END:
        blocks.append([parent_of[first + s] * SEG for s in range(4)])
    return blocks


def seg_dot(rows, keys_ref, starts):
    return jnp.concatenate(
        [
            contract_cols(rows[s * SEG : (s + 1) * SEG], keys_ref[pl.ds(starts[s], SEG), :])
            for s in range(4)
        ],
        0,
    )


def chunk_weights(chunk, query, k_ref, blocks, scale):
    pieces = []
    if chunk == 0:
        score = contract_cols(query, k_ref[0:TRUNK, :]) * scale
        pieces.append(jnp.where(causal(TRUNK), score, NEGATIVE))
    else:
        if TRUNK * chunk < LEAF_END:
            pieces.append(contract_cols(query, k_ref[0:TRUNK, :]) * scale)
        mask = jnp.concatenate([causal(SEG)] * 4, 0)
        pieces.append(jnp.where(mask, seg_dot(query, k_ref, blocks[0]) * scale, NEGATIVE))
        for starts in blocks[1:]:
            pieces.append(seg_dot(query, k_ref, starts) * scale)
    highest = jnp.max(pieces[0], -1, keepdims=True)
    for piece in pieces[1:]:
        highest = jnp.maximum(highest, jnp.max(piece, -1, keepdims=True))
    raised = [jnp.exp(piece - highest) for piece in pieces]
    total = jnp.sum(raised[0], -1, keepdims=True)
    for piece in raised[1:]:
        total = total + jnp.sum(piece, -1, keepdims=True)
    inverse = 1.0 / total
    return [piece * inverse for piece in raised]


def chunk_parts(chunk, pieces, blocks):
    places = []
    if chunk == 0:
        places = [None]
    else:
        if TRUNK * chunk < LEAF_END:
            places.append(None)
        places = places + blocks
    return list(zip(pieces, places))


def forward_kernel(
    parents_ref,
    q_ref,
    k_ref,
    v_ref,
    qs_ref,
    ks_ref,
    qg_ref,
    kg_ref,
    cos_ref,
    sin_ref,
    att_ref,
    qr_ref,
    kr_ref,
    vl_ref,
):
    tree = pl.program_id(0)
    scale = 1.0 / math.sqrt(HD)
    parent_of = [parents_ref[tree, s] for s in range(NSEG)]

    def turned(field):
        return field * cos_ref[...] + pltpu.roll(field, HD // 2, 1) * sin_ref[...]

    qr_ref[...] = turned(q_ref[...] * qs_ref[...] * qg_ref[...]).astype(jnp.bfloat16)
    kr_ref[...] = turned(k_ref[...] * ks_ref[...] * kg_ref[...]).astype(jnp.bfloat16)
    vl_ref[...] = v_ref[...].astype(jnp.bfloat16)
    for chunk in range(TREE // TRUNK):
        rows = slice(chunk * TRUNK, (chunk + 1) * TRUNK)
        blocks = key_starts(chunk, parent_of)
        weights = chunk_weights(chunk, qr_ref[rows, :], kr_ref, blocks, scale)
        total = jnp.zeros((TRUNK, HD), jnp.float32)
        for weight, starts in chunk_parts(chunk, weights, blocks):
            low = weight.astype(jnp.bfloat16)
            if starts is None:
                total = total + dot_f32(low, vl_ref[0:TRUNK, :], 1, 0)
            else:
                total = total + jnp.concatenate(
                    [
                        dot_f32(
                            low[s * SEG : (s + 1) * SEG], vl_ref[pl.ds(starts[s], SEG), :], 1, 0
                        )
                        for s in range(4)
                    ],
                    0,
                )
        att_ref[rows, :] = total.astype(jnp.bfloat16)


def backward_kernel(
    parents_ref,
    qr_ref,
    kr_ref,
    vl_ref,
    do_ref,
    cos_ref,
    sin_ref,
    dq_ref,
    dk_ref,
    dv_ref,
    dv_acc,
):
    tree = pl.program_id(0)
    scale = 1.0 / math.sqrt(HD)
    parent_of = [parents_ref[tree, s] for s in range(NSEG)]
    dk_ref[...] = jnp.zeros_like(dk_ref)
    dv_acc[...] = jnp.zeros_like(dv_acc)
    for chunk in range(TREE // TRUNK):
        rows = slice(chunk * TRUNK, (chunk + 1) * TRUNK)
        blocks = key_starts(chunk, parent_of)
        query = qr_ref[rows, :]
        grad = do_ref[rows, :]
        weights = chunk_weights(chunk, query, kr_ref, blocks, scale)
        parts = chunk_parts(chunk, weights, blocks)
        d_weights = []
        row_dot = jnp.zeros((TRUNK, 1), jnp.float32)
        for weight, starts in parts:
            if starts is None:
                d_weight = contract_cols(grad, vl_ref[0:TRUNK, :])
            else:
                d_weight = seg_dot(grad, vl_ref, starts)
            d_weights.append(d_weight)
            row_dot = row_dot + jnp.sum(weight * d_weight, -1, keepdims=True)
        d_query = jnp.zeros((TRUNK, HD), jnp.float32)
        for (weight, starts), d_weight in zip(parts, d_weights):
            low = weight.astype(jnp.bfloat16)
            d_score = (weight * (d_weight - row_dot)).astype(jnp.bfloat16)
            if starts is None:
                d_query = d_query + dot_f32(d_score, kr_ref[0:TRUNK, :], 1, 0)
                dk_ref[0:TRUNK, :] += contract_rows(d_score, query)
                dv_acc[0:TRUNK, :] += contract_rows(low, grad)
            else:
                turns = []
                for s in range(4):
                    own = slice(s * SEG, (s + 1) * SEG)
                    keys = pl.ds(starts[s], SEG)
                    turns.append(dot_f32(d_score[own], kr_ref[keys, :], 1, 0))
                    dk_ref[keys, :] += contract_rows(d_score[own], query[own])
                    dv_acc[keys, :] += contract_rows(low[own], grad[own])
                d_query = d_query + jnp.concatenate(turns, 0)
        dq_ref[rows, :] = d_query

    def unturned(field):
        return (field * cos_ref[...] - pltpu.roll(field, HD // 2, 1) * sin_ref[...]) * scale

    dq_ref[...] = unturned(dq_ref[...])
    dk_ref[...] = unturned(dk_ref[...])
    dv_ref[...] = dv_acc[...].astype(jnp.bfloat16)


def attend(parents, qkv, q_scale, k_scale, q_gain, k_gain, cos_table, sin_table, heads):
    trees = parents.shape[0]
    rows = qkv.shape[0]

    def field(shift):
        return pl.BlockSpec((TREE, HD), lambda t, h, p: (t, h + shift))

    scale_spec = pl.BlockSpec((TREE, 1), lambda t, h, p: (t, 0))
    gain_spec = pl.BlockSpec((1, HD), lambda t, h, p: (0, h))
    table = pl.BlockSpec((TREE, HD), lambda t, h, p: (t, 0))
    return pl.pallas_call(
        forward_kernel,
        grid_spec=pltpu.PrefetchScalarGridSpec(
            num_scalar_prefetch=1,
            grid=(trees, heads),
            in_specs=[
                field(0),
                field(heads),
                field(2 * heads),
                scale_spec,
                scale_spec,
                gain_spec,
                gain_spec,
                table,
                table,
            ],
            out_specs=[field(0)] * 4,
        ),
        out_shape=[jax.ShapeDtypeStruct((rows, heads * HD), jnp.bfloat16)] * 4,
        compiler_params=pltpu.CompilerParams(vmem_limit_bytes=50 * MIB),
        name="tree_forward",
    )(
        parents,
        qkv,
        qkv,
        qkv,
        q_scale,
        k_scale,
        q_gain[None, :],
        k_gain[None, :],
        cos_table,
        sin_table,
    )


def attend_back(parents, q_rot, k_rot, values, d_attended, cos_table, sin_table, heads):
    trees = parents.shape[0]
    rows = q_rot.shape[0]
    field = pl.BlockSpec((TREE, HD), lambda t, h, p: (t, h))
    table = pl.BlockSpec((TREE, HD), lambda t, h, p: (t, 0))
    return pl.pallas_call(
        backward_kernel,
        grid_spec=pltpu.PrefetchScalarGridSpec(
            num_scalar_prefetch=1,
            grid=(trees, heads),
            in_specs=[field, field, field, field, table, table],
            out_specs=[field] * 3,
            scratch_shapes=[pltpu.VMEM((TREE, HD), jnp.float32)],
        ),
        out_shape=[
            jax.ShapeDtypeStruct((rows, heads * HD), jnp.float32),
            jax.ShapeDtypeStruct((rows, heads * HD), jnp.float32),
            jax.ShapeDtypeStruct((rows, heads * HD), jnp.bfloat16),
        ],
        compiler_params=pltpu.CompilerParams(vmem_limit_bytes=50 * MIB),
        name="tree_backward",
    )(parents, q_rot, k_rot, values, d_attended, cos_table, sin_table)


def slots_kernel(slot_ref, gate_ref, gain_ref, x_ref, *refs, normed):
    units = slot_ref.shape[1]
    outs, gate_out, acc, gate_acc = refs[:units], refs[units], refs[units + 1], refs[units + 2]
    step = pl.program_id(1)

    @pl.when(step == 0)
    def _():
        acc[...] = jnp.zeros_like(acc)
        gate_acc[...] = jnp.zeros_like(gate_acc)

    for e in range(units):
        slots = lax.broadcasted_iota(jnp.int32, (CAPP, x_ref.shape[0]), 0)
        picks = slot_ref[0, e : e + 1, :] == slots
        acc[e] += dot_f32(picks.astype(jnp.bfloat16), x_ref[...], 1, 0)
        gate_acc[e] += jnp.sum(jnp.where(picks, gate_ref[0, e : e + 1, :], 0.0), 1, keepdims=True)

    @pl.when(step == pl.num_programs(1) - 1)
    def _():
        for e in range(units):
            rows = acc[e]
            if normed:
                scale = lax.rsqrt(jnp.mean(rows * rows, 1, keepdims=True) + EPS)
                outs[e][...] = (rows * scale * gain_ref[...]).astype(jnp.bfloat16)
            else:
                outs[e][...] = (gate_acc[e] * rows).astype(jnp.bfloat16)
            gate_out[e] = gate_acc[e]


def to_slots(slot_of, token_gate, gain, rows, normed):
    groups, units, tok_rows = slot_of.shape
    width = rows.shape[1]
    block = tok_rows // 2
    steps = tok_rows // block
    table = pl.BlockSpec((1, units, block), lambda g, t: (g, 0, t))
    out = pl.pallas_call(
        functools.partial(slots_kernel, normed=normed),
        grid=(groups, steps),
        in_specs=[
            table,
            table,
            pl.BlockSpec((1, width), lambda g, t: (0, 0)),
            pl.BlockSpec((block, width), lambda g, t: (g * steps + t, 0)),
        ],
        out_specs=[pl.BlockSpec((CAPP, width), lambda g, t: (g, 0))] * units
        + [pl.BlockSpec((units, CAPP, 1), lambda g, t: (0, g, 0))],
        out_shape=[jax.ShapeDtypeStruct((groups * CAPP, width), jnp.bfloat16)] * units
        + [jax.ShapeDtypeStruct((units, groups * CAPP, 1), jnp.float32)],
        scratch_shapes=[
            pltpu.VMEM((units, CAPP, width), jnp.float32),
            pltpu.VMEM((units, CAPP, 1), jnp.float32),
        ],
        compiler_params=pltpu.CompilerParams(vmem_limit_bytes=56 * MIB),
        cost_estimate=pl.CostEstimate(
            flops=2 * groups * tok_rows * units * CAPP * width,
            bytes_accessed=2 * groups * tok_rows * width,
            transcendentals=0,
        ),
        name="slots",
    )(slot_of, token_gate, gain[None, :], rows)
    return out[:units], out[units]


def combine_kernel(slot_ref, *refs):
    out_ref = refs[-1]
    total = None
    for e, y_ref in enumerate(refs[:-1]):
        slots = lax.broadcasted_iota(jnp.int32, (slot_ref.shape[0], CAPP), 1)
        picks = (slot_ref[:, e : e + 1] == slots).astype(jnp.bfloat16)
        term = dot_f32(picks, y_ref[0], 1, 0)
        total = term if total is None else total + term
    out_ref[...] = total.astype(out_ref.dtype)


def combine(slot_of, slot_rows, tok_rows, half=None):
    units, width = len(slot_rows), slot_rows[0].shape[1]
    groups = slot_rows[0].shape[0] // CAPP
    block = tok_rows // 4
    steps = 4 if half is None else 2
    first = 0 if half is None else 2 * half
    rows_spec = pl.BlockSpec((1, CAPP, width), lambda g, t: (g, 0, 0))
    return pl.pallas_call(
        combine_kernel,
        grid=(groups, steps),
        in_specs=[pl.BlockSpec((block, units), lambda g, t: (g * 4 + first + t, 0))]
        + [rows_spec] * units,
        out_specs=pl.BlockSpec((block, width), lambda g, t: (g * steps + t, 0)),
        out_shape=jax.ShapeDtypeStruct((groups * steps * block, width), jnp.bfloat16),
        compiler_params=pltpu.CompilerParams(vmem_limit_bytes=50 * MIB),
        cost_estimate=pl.CostEstimate(
            flops=2 * groups * steps * block * units * CAPP * width,
            bytes_accessed=2 * groups * steps * block * width,
            transcendentals=0,
        ),
        name="combine",
    )(slot_of, *[rows.reshape(groups, CAPP, width) for rows in slot_rows])


def shift_row(block, k):
    count = lax.axis_size("row")
    return lax.ppermute(block, "row", [(i, (i + k) % count) for i in range(count)])


def row_stack(part, *earlier):
    count = lax.axis_size("row")
    here = lax.axis_index("row")
    part = after(part, *earlier)
    whole = jnp.zeros((count,) + part.shape, part.dtype)
    for k in range(count):
        block = part if k == 0 else shift_row(part, k)
        whole = lax.dynamic_update_slice_in_dim(whole, block[None], (here - k) % count, 0)
    return whole


def crossing_units():
    count = lax.axis_size("row")
    units = []
    for k in range(1, count):
        parts = 1 if k in (1, count - 1) else 2
        units = units + [(k, part, parts) for part in range(parts)]
    return units


def home_unit(weight, unit, *earlier):
    k, part, parts = unit
    groups = lax.axis_size("row")
    share = weight.shape[1] // groups
    to = (lax.axis_index("row") + k) % groups
    block = lax.dynamic_slice_in_dim(
        after(weight, *earlier), to * share + part * (share // parts), share // parts, 1
    )
    return shift_row(block, k)


def home_kernel(here_ref, own_ref, *refs, units, groups):
    out_ref = refs[-1]
    source = lax.rem(here_ref[0] - pl.program_id(0) + groups, groups)

    @pl.when(source == 0)
    def _():
        out_ref[...] = own_ref[...]

    for (k, part, parts), block_ref in zip(units, refs[:-1]):
        wide = out_ref.shape[1] // parts

        @pl.when(source == k)
        def _(block_ref=block_ref, start=part * wide, wide=wide):
            out_ref[:, start : start + wide] = block_ref[...]


def at_home(weight, units, blocks):
    groups = lax.axis_size("row")
    depth, columns = weight.shape
    share = columns // groups
    return pl.pallas_call(
        functools.partial(home_kernel, units=units, groups=groups),
        grid_spec=pltpu.PrefetchScalarGridSpec(
            num_scalar_prefetch=1,
            grid=(groups,),
            in_specs=[pl.BlockSpec((depth, share), lambda j, here: (0, here[0]))]
            + [pl.BlockSpec(block.shape, lambda j, here: (0, 0)) for block in blocks],
            out_specs=pl.BlockSpec((depth, share), lambda j, here: (j, 0)),
        ),
        out_shape=jax.ShapeDtypeStruct((depth * groups, share), weight.dtype),
        compiler_params=pltpu.CompilerParams(vmem_limit_bytes=50 * MIB),
        cost_estimate=pl.CostEstimate(
            flops=0, bytes_accessed=4 * depth * columns, transcendentals=0
        ),
        name="at_home",
    )(lax.axis_index("row").astype(jnp.int32)[None], weight, *blocks)


def back_units(count):
    rows = lax.axis_size("row")
    units = []
    for k in range(1, rows):
        if k in (1, rows - 1):
            units.append((k, tuple(range(count))))
        else:
            units = units + [(k, (e,)) for e in range(count)]
    return units


def back_unit(grads, unit, *earlier):
    k, which = unit
    groups = lax.axis_size("row")
    depth = grads[0].shape[0] // groups
    to = (lax.axis_index("row") + k) % groups
    chosen = after([grads[e] for e in which], *earlier)
    return [
        shift_row(lax.dynamic_slice_in_dim(grad, to * depth, depth, 0), k) for grad in chosen
    ]


def owner_kernel(here_ref, *refs, units, groups, count):
    out_ref = refs[-1]
    hidden = refs[0].shape[1]
    source = lax.rem(here_ref[0] - pl.program_id(0) + groups, groups)
    places = [(0, e) for e in range(count)]
    places = places + [(k, e) for k, which in units for e in which]
    for (k, e), block_ref in zip(places, refs[:-1]):

        @pl.when(source == k)
        def _(block_ref=block_ref, start=e * hidden):
            out_ref[:, start : start + hidden] = block_ref[...].astype(jnp.float32)


def at_owner(grads, units, received):
    groups = lax.axis_size("row")
    depth, hidden = grads[0].shape[0] // groups, grads[0].shape[1]
    count = len(grads)
    share = hidden * count
    blocks = [block for pair in received for block in pair]
    return pl.pallas_call(
        functools.partial(owner_kernel, units=units, groups=groups, count=count),
        grid_spec=pltpu.PrefetchScalarGridSpec(
            num_scalar_prefetch=1,
            grid=(groups,),
            in_specs=[pl.BlockSpec((depth, hidden), lambda j, here: (here[0], 0))] * count
            + [pl.BlockSpec((depth, hidden), lambda j, here: (0, 0))] * len(blocks),
            out_specs=pl.BlockSpec((depth, share), lambda j, here: (0, j)),
        ),
        out_shape=jax.ShapeDtypeStruct((depth, share * groups), jnp.float32),
        compiler_params=pltpu.CompilerParams(vmem_limit_bytes=50 * MIB),
        cost_estimate=pl.CostEstimate(
            flops=0, bytes_accessed=6 * depth * share * groups, transcendentals=0
        ),
        name="at_owner",
    )(lax.axis_index("row").astype(jnp.int32)[None], *grads, *blocks)


def line_steps(part, *earlier):
    count = lax.axis_size("row")
    upward = downward = part
    steps = []
    for _ in range(count - 1):
        upward, downward = after((upward, downward), *earlier)
        upward = lax.ppermute(upward, "row", [(i, i + 1) for i in range(count - 1)])
        downward = lax.ppermute(downward, "row", [(i + 1, i) for i in range(count - 1)])
        earlier = (upward, downward)
        steps.append((upward, downward))
    return steps


def line_gather(part, steps):
    count = lax.axis_size("row")
    here = lax.axis_index("row")
    rows = part.shape[0]
    whole = jnp.zeros((rows * count, part.shape[1]), part.dtype)
    whole = lax.dynamic_update_slice_in_dim(whole, part, here * rows, 0)
    for k in range(1, count):
        block = jnp.where(here >= k, steps[k - 1][0], steps[count - k - 1][1])
        whole = lax.dynamic_update_slice_in_dim(whole, block, ((here - k) % count) * rows, 0)
    return whole


def group_total(part, along=(), beside=None):
    groups = lax.axis_size("row")
    here = lax.axis_index("row")
    rows = part.shape[0] // groups

    def rows_of(group):
        start = jnp.clip(group, 0, groups - 1) * rows
        return lax.dynamic_slice_in_dim(part, start, rows, 0).astype(jnp.float32)

    upward = downward = 0.0
    for step in range(1, groups):
        upward = (rows_of(here + groups - step) + upward).astype(jnp.bfloat16)
        downward = (rows_of(here - groups + step) + downward).astype(jnp.bfloat16)
        upward = lax.ppermute(upward, "row", [(i, i + 1) for i in range(step)])
        downward = lax.ppermute(downward, "row", [(groups - 1 - i, groups - 2 - i) for i in range(step)])
        ties = along if step == groups - 2 else ()
        if step == groups - 1 and beside is not None:
            ties = beside()
        upward, downward = after((upward, downward), *ties)
        upward, downward = upward.astype(jnp.float32), downward.astype(jnp.float32)
    return rows_of(here) + upward + downward


def body(
    tokens,
    attn_norm,
    w_query,
    w_key,
    w_value,
    q_norm,
    k_norm,
    w_out,
    moe_norm,
    w_gate,
    w_up,
    w_down,
    routes,
    gates,
    parents,
    cotangent,
):
    tok_rows, own_width = tokens.shape
    groups = lax.axis_size("row")
    cols = lax.axis_size("col")
    width = own_width * cols
    here, col = lax.axis_index("row"), lax.axis_index("col")
    col_start = col * own_width
    heads = own_width // HD
    trees = parents.shape[0]

    qkv_cols = lax.all_gather(
        jnp.concatenate([w_query, w_key, w_value], 1), "row", axis=0, tiled=True
    )
    out_cols = lax.all_gather(after(w_out, qkv_cols), "row", axis=0, tiled=True)
    shifts = crossing_units()
    last = len(shifts) - 1
    grad_steps = line_steps(cotangent, qkv_cols)

    wide = jnp.concatenate(gather_blocks(tokens), 1).astype(jnp.float32)
    cos_table, sin_table = jax.vmap(rope_tables)(parents)
    cos_table, sin_table = cos_table.reshape(-1, HD), sin_table.reshape(-1, HD)
    scale_one = lax.rsqrt(jnp.mean(wide * wide, 1, keepdims=True) + EPS)
    norm_gain = block_order(attn_norm, own_width)
    normed_one = (wide * scale_one * norm_gain[None, :]).astype(jnp.bfloat16)
    qkv_cols = block_order(qkv_cols, own_width)
    qkv = jnp.dot(normed_one, qkv_cols, preferred_element_type=jnp.float32)
    query, keyed = qkv[:, :own_width], qkv[:, own_width : 2 * own_width]
    squares = over_col(jnp.stack([jnp.sum(query * query, 1), jnp.sum(keyed * keyed, 1)]))
    q_scale = lax.rsqrt(squares[0] / width + EPS)[:, None]
    k_scale = lax.rsqrt(squares[1] / width + EPS)[:, None]
    q_gain = lax.dynamic_slice_in_dim(q_norm, col_start, own_width)
    k_gain = lax.dynamic_slice_in_dim(k_norm, col_start, own_width)
    q_scale = after(q_scale, grad_steps[0])
    attended, q_rot, k_rot, value_low = attend(
        parents, qkv, q_scale, k_scale, q_gain, k_gain, cos_table, sin_table, heads
    )
    attn_sum = lax.psum_scatter(
        after(contract_cols(attended, out_cols).astype(jnp.bfloat16), grad_steps[:-1]),
        "col",
        scatter_dimension=1,
        tiled=True,
    )
    route_all = row_stack(routes.T, grad_steps[:-1])
    gate_all = row_stack(gates.T, grad_steps[:-1])
    gate_units = [home_unit(w_gate, shifts[0], grad_steps[:-1])]
    attn_sum = after(attn_sum, gate_units, grad_steps, route_all, gate_all)
    residual = tokens.astype(jnp.float32) + attn_sum.astype(jnp.float32)
    mid_low = residual.astype(jnp.bfloat16)
    mid_own = mid_low.astype(jnp.float32)
    mid_row = lax.all_gather(mid_low, "row", axis=0, tiled=True)
    gate_units.append(home_unit(w_gate, shifts[1], mid_low))
    grad_row = line_gather(cotangent, grad_steps)

    share = w_gate.shape[1] // groups
    units, hidden_units = max(1, share // FF), min(share, FF)
    first_unit = col * (w_gate.shape[1] // FF) + (here * share) // FF
    unit_ids = first_unit + jnp.arange(units, dtype=jnp.int32)
    match = route_all[None] == unit_ids[:, None, None, None]
    named = jnp.any(match, 2)
    token_gate = jnp.sum(jnp.where(match, gate_all[None], 0.0), 2)
    rank = jnp.cumsum(named.astype(jnp.int32), 2) - 1
    slot_of = jnp.where(named, rank, -1)
    slot_of, token_gate = slot_of.transpose(1, 0, 2), token_gate.transpose(1, 0, 2)
    slot_column = slot_of.transpose(0, 2, 1).reshape(groups * tok_rows, units)
    mid_row, slot_of, token_gate, slot_column, grad_row = after(
        (mid_row, slot_of, token_gate, slot_column, grad_row), gate_units
    )
    mid_all = lax.all_gather(mid_row, "col", axis=1, tiled=True)
    scale_two = lax.rsqrt(over_col(jnp.sum(mid_own * mid_own, 1)) / width + EPS)[:, None]
    for unit in shifts[2:]:
        gate_units.append(home_unit(w_gate, unit, gate_units[-1], mid_row))
    gate_home = at_home(w_gate, shifts, gate_units)
    up_units = [home_unit(w_up, shifts[0], gate_units[-1])]
    for unit in shifts[1:last]:
        up_units.append(home_unit(w_up, unit, up_units[-1]))
    mid_all, gate_home = after((mid_all, gate_home), up_units[-2])
    grad_all = lax.all_gather(after(grad_row, mid_all), "col", axis=1, tiled=True)

    experts = range(units)
    cut = [slice(e * hidden_units, (e + 1) * hidden_units) for e in experts]
    expert_in, slot_gate = to_slots(slot_of, token_gate, moe_norm, mid_all, True)
    expert_in = after(expert_in, up_units[-1])
    up_units = after(up_units, expert_in)
    up_units.append(home_unit(w_up, shifts[last], up_units[-1], expert_in))
    gate_acts = [dot_f32(expert_in[e], gate_home[:, cut[e]], 1, 0) for e in experts]
    up_home, gate_acts = after((at_home(w_up, shifts, up_units), gate_acts))
    down_units = [home_unit(w_down, shifts[0], up_home)]
    acts = []
    for e in experts:
        up_act = dot_f32(expert_in[e], up_home[:, cut[e]], 1, 0)
        sigmoid_gate = jax.nn.sigmoid(gate_acts[e])
        silu_gate = gate_acts[e] * sigmoid_gate
        hidden = (silu_gate * up_act).astype(jnp.bfloat16)
        acts.append((gate_acts[e], up_act, sigmoid_gate, silu_gate, hidden))
    hiddens = after([act[-1] for act in acts], down_units[0])
    down_units.append(home_unit(w_down, shifts[1], hiddens))
    grad_all = after(grad_all, down_units[1])
    for unit in shifts[2:last]:
        down_units.append(home_unit(w_down, unit, grad_all))
    d_out, _ = to_slots(slot_of, token_gate, moe_norm, grad_all, False)
    d_out = after(d_out, down_units[-1])
    down_units.append(home_unit(w_down, shifts[last], d_out))
    leaving = back_units(units)
    early, late = leaving[1:2], [leaving[0]] + leaving[2:]
    down_grads = [contract_rows(d_out[0], hiddens[0]).astype(jnp.bfloat16)]
    down_grads, d_out, hiddens, down_units = after((down_grads, d_out, hiddens, down_units))
    down_back = [back_unit(down_grads, unit) for unit in early]
    for e in experts[1:]:
        down_grads.append(contract_rows(d_out[e], hiddens[e]).astype(jnp.bfloat16))
    down_home = at_home(w_down, shifts, down_units)
    down_grads, down_home, d_out = after((down_grads, down_home, d_out))

    d_acts, terms = [], []
    for e in experts:
        gate_act, up_act, sigmoid_gate, silu_gate, _ = acts[e]
        d_hidden = dot_f32(d_out[e], down_home[:, cut[e]], 1, 0)
        d_gate = (
            d_hidden * up_act * sigmoid_gate * (1.0 + gate_act * (1.0 - sigmoid_gate))
        ).astype(jnp.bfloat16)
        d_acts.append((d_gate, (d_hidden * silu_gate).astype(jnp.bfloat16)))
        terms.append(contract_cols(d_gate, gate_home[:, cut[e]]))
        if e == 0:
            terms, d_acts, d_out = after((terms, d_acts, d_out), down_back)
            down_back.append(back_unit(down_grads, late[0], terms))
    terms, d_acts = after((terms, d_acts), down_back)
    for unit in late[1:-1]:
        down_back.append(back_unit(down_grads, unit, terms))
    d_in = [
        (terms[e] + contract_cols(d_acts[e][1], up_home[:, cut[e]])).astype(jnp.bfloat16)
        for e in experts
    ]
    d_rows = combine(slot_column, d_in, tok_rows)
    d_rows, expert_in, d_acts = after((d_rows, expert_in, d_acts), down_back)
    down_back.append(back_unit(down_grads, late[-1], d_rows))
    d_rows = lax.psum_scatter(d_rows, "col", scatter_dimension=1, tiled=True)
    gate_grads = [contract_rows(expert_in[e], d_acts[e][0]).astype(jnp.bfloat16) for e in experts]
    up_grads = [contract_rows(expert_in[e], d_acts[e][1]).astype(jnp.bfloat16) for e in experts]
    gate_grads, up_grads, hiddens = after((gate_grads, up_grads, hiddens), down_back[-1])
    gate_back = [back_unit(gate_grads, leaving[0])]
    gate_back.append(back_unit(gate_grads, leaving[1]))
    gated = [
        (slot_gate[e] * contract_cols(hiddens[e], down_home[:, cut[e]])).astype(jnp.bfloat16)
        for e in experts
    ]
    halves = [combine(slot_column, gated, tok_rows, half) for half in (0, 1)]
    halves = after(halves, gate_back)
    for unit in leaving[2:]:
        gate_back.append(back_unit(gate_grads, unit, halves))
    d_rows = after(d_rows, gate_back)
    up_back = [back_unit(up_grads, leaving[0], d_rows)]
    d_normed_two = group_total(d_rows, up_back[0])
    halves[0] = lax.psum_scatter(
        after(halves[0], d_rows), "col", scatter_dimension=1, tiled=True
    )
    w_down_grad = at_owner(down_grads, early + late, down_back)
    w_gate_grad = at_owner(gate_grads, leaving, gate_back)

    gain_two = lax.dynamic_slice_in_dim(moe_norm, col_start, own_width)
    moe_dot = over_col(jnp.sum(d_normed_two * gain_two * mid_own, 1))
    d_residual = (
        cotangent.astype(jnp.float32)
        + scale_two * gain_two * d_normed_two
        - mid_own * scale_two**3 * (moe_dot / width)[:, None]
    )
    moe_gain_grad = jnp.sum(d_normed_two * mid_own * scale_two, 0)
    d_res_low = d_residual.astype(jnp.bfloat16)
    up_back.append(back_unit(up_grads, leaving[1], d_normed_two))
    d_res_low, halves[0], w_down_grad = after((d_res_low, halves[0], w_down_grad))
    d_attn_whole = lax.all_gather(d_res_low, "col", axis=1, tiled=True)
    d_attn_whole, w_gate_grad = after((d_attn_whole, w_gate_grad), up_back)
    halves[1] = lax.psum_scatter(
        after(halves[1], d_attn_whole), "col", scatter_dimension=1, tiled=True
    )
    moe_sums = [group_total(after(halves[0], d_attn_whole))]
    d_attended = jnp.dot(
        d_attn_whole, out_cols, preferred_element_type=jnp.float32
    ).astype(jnp.bfloat16)
    d_qn, d_kn, d_values = attend_back(
        parents, q_rot, k_rot, value_low, d_attended, cos_table, sin_table, heads
    )
    qk_dots = over_col(
        jnp.stack([jnp.sum(query * q_gain * d_qn, 1), jnp.sum(keyed * k_gain * d_kn, 1)])
    )
    up_back.append(back_unit(up_grads, leaving[2], d_attn_whole))
    qk_dots = after(qk_dots, moe_sums[0], up_back)
    for unit in leaving[3:]:
        up_back.append(back_unit(up_grads, unit, up_back[2], qk_dots))
    d_query = (
        q_scale * q_gain * d_qn - query * q_scale**3 * (qk_dots[0] / width)[:, None]
    ).astype(jnp.bfloat16)
    d_keyed = (
        k_scale * k_gain * d_kn - keyed * k_scale**3 * (qk_dots[1] / width)[:, None]
    ).astype(jnp.bfloat16)
    q_gain_grad = jnp.sum(d_qn * query * q_scale, 0)
    k_gain_grad = jnp.sum(d_kn * keyed * k_scale, 0)
    d_qkv = jnp.concatenate([d_query, d_keyed, d_values], 1)
    d_one = block_order(contract_cols(qkv_cols, d_qkv).astype(jnp.bfloat16), own_width)
    d_qkv, attended, d_attn_whole = after((d_qkv, attended, d_attn_whole), d_one)
    attn_grads = jnp.concatenate(
        [
            block_order(contract_rows(normed_one, d_qkv).astype(jnp.bfloat16), own_width),
            contract_rows(d_attn_whole, attended).astype(jnp.bfloat16),
        ],
        1,
    )
    d_one, attn_grads, halves[1] = after((d_one, attn_grads, halves[1]), up_back[-1])
    w_up_grad = at_owner(up_grads, leaving, up_back)
    d_normed_one = lax.psum_scatter(d_one, "col", scatter_dimension=0, tiled=True)
    attn_grads = group_total(attn_grads)
    d_normed_one = d_normed_one.astype(jnp.float32).T
    w_query_grad = attn_grads[:, :own_width]
    w_key_grad = attn_grads[:, own_width : 2 * own_width]
    w_value_grad = attn_grads[:, 2 * own_width : 3 * own_width]
    w_out_grad = attn_grads[:, 3 * own_width :]
    tokens_own = tokens.astype(jnp.float32)
    gain_one = lax.dynamic_slice_in_dim(attn_norm, col_start, own_width)
    attn_dot = over_col(jnp.sum(d_normed_one * gain_one * tokens_own, 1))
    tokens_grad = (
        d_residual
        + scale_one * gain_one * d_normed_one
        - tokens_own * scale_one**3 * (attn_dot / width)[:, None]
    )
    attn_gain_grad = jnp.sum(d_normed_one * tokens_own * scale_one, 0)
    gain_grads = jnp.sum(
        row_stack(jnp.stack([attn_gain_grad, q_gain_grad, k_gain_grad, moe_gain_grad])), 0
    )
    moe_sums.append(group_total(halves[1], beside=lambda: (gain_grads, tokens_grad, w_up_grad)))
    moe_sum = jnp.concatenate(moe_sums, 0)
    output = (residual + moe_sum).astype(jnp.bfloat16)
    return (
        output,
        tokens_grad,
        gain_grads[0],
        w_query_grad,
        w_key_grad,
        w_value_grad,
        gain_grads[1],
        gain_grads[2],
        w_out_grad,
        gain_grads[3],
        w_gate_grad,
        w_up_grad,
        w_down_grad,
    )


def solution(mesh):
    grid = P("row", "col")
    rows = P("row", None)
    in_specs = (
        grid,
        P(),
        grid,
        grid,
        grid,
        P(),
        P(),
        grid,
        P(),
        grid,
        grid,
        grid,
        rows,
        rows,
        rows,
        grid,
    )
    out_specs = (
        grid,
        grid,
        P("col"),
        grid,
        grid,
        grid,
        P("col"),
        P("col"),
        grid,
        P("col"),
        grid,
        grid,
        grid,
    )
    return jax.shard_map(body, mesh=mesh, in_specs=in_specs, out_specs=out_specs, check_vma=False)
```

```python
import functools
import math

import jax
import jax.numpy as jnp
from jax import lax
from jax.experimental import pallas as pl
from jax.experimental.pallas import tpu as pltpu
from jax.sharding import PartitionSpec as P

HD = 128
FF = 1024
SEG = 128
TREE = 2560
NSEG = 20
TRUNK = 512
BRANCH_END = 1024
LEAF_END = 2048
CAP = 426
CAPP = 432


EPS = 1e-05
NEGATIVE = -1e30
MIB = 1024 * 1024


def depths_of(parent_ids):
    segment_ids = jnp.arange(NSEG, dtype=jnp.int32)

    def advance(turn_index, loop_state):
        current, depth = loop_state
        matches = current[:, None] == segment_ids[None, :]
        parent_of = jnp.sum(jnp.where(matches, parent_ids[None, :], 0), 1)
        current = jnp.where(current >= 0, parent_of, -1)
        return (current, depth + (current >= 0).astype(jnp.int32))

    start = (segment_ids, jnp.zeros((NSEG,), jnp.int32))
    state = start
    for turn in range(6):
        state = advance(turn, state)
    return state[1]


def rope_tables(parent_ids):
    depths = depths_of(parent_ids)
    position = jnp.arange(TREE, dtype=jnp.int32)
    places = (jnp.repeat(depths, SEG) * SEG + position % SEG).astype(jnp.float32)
    frequency = jnp.exp(jnp.arange(HD // 2, dtype=jnp.float32) * (-2.0 * math.log(10000.0) / HD))
    angles = places[:, None] * frequency[None, :]
    cosine, sine = jnp.cos(angles), jnp.sin(angles)
    return (
        jnp.concatenate([cosine, cosine], -1),
        jnp.concatenate([-sine, sine], -1),
    )


def dot_f32(left, right, left_dim, right_dim):
    return lax.dot_general(
        left, right, (((left_dim,), (right_dim,)), ((), ())), preferred_element_type=jnp.float32
    )


def contract_rows(left, right):
    return dot_f32(left, right, 0, 0)


def contract_cols(left, right):
    return dot_f32(left, right, 1, 1)


def over_col(partial_value):
    return jnp.sum(lax.all_gather(partial_value, "col", axis=0), 0)


def after(value, *earlier):
    return lax.optimization_barrier((value,) + earlier)[0]


def gather_blocks(part):
    count = lax.axis_size("col")

    def swap(block, bits):
        return lax.ppermute(block, "col", [(i, i ^ bits) for i in range(count)])

    if count == 8:
        half = part.shape[0] // 2
        side, far, twin = swap(part, 2), swap(part, 4), swap(part, 1)
        corner = jnp.concatenate([swap(far[:half], 2), swap(side[half:], 4)], 0)
        return [
            part,
            twin,
            side,
            swap(side, 1),
            far,
            swap(far, 1),
            corner,
            swap(corner, 1),
        ]
    blocks = [part]
    bits = 1
    while bits < count:
        blocks = blocks + [swap(block, bits) for block in blocks]
        bits = bits * 2
    return blocks


def block_order(rows, depth):
    own = lax.axis_index("col")
    count = rows.shape[0] // depth
    return jnp.concatenate(
        [lax.dynamic_slice_in_dim(rows, (own ^ k) * depth, depth, 0) for k in range(count)], 0
    )


def causal(count):
    rows = lax.broadcasted_iota(jnp.int32, (count, count), 0)
    cols = lax.broadcasted_iota(jnp.int32, (count, count), 1)
    return cols <= rows


def key_starts(chunk, parent_of):
    first = chunk * 4
    blocks = [[(first + s) * SEG for s in range(4)]]
    if TRUNK * chunk >= BRANCH_END and TRUNK * chunk < LEAF_END:
        blocks.append([parent_of[first + s] * SEG for s in range(4)])
    return blocks


def seg_dot(rows, keys_ref, starts):
    return jnp.concatenate(
        [
            contract_cols(rows[s * SEG : (s + 1) * SEG], keys_ref[pl.ds(starts[s], SEG), :])
            for s in range(4)
        ],
        0,
    )


def chunk_weights(chunk, query, k_ref, blocks, scale):
    pieces = []
    if chunk == 0:
        score = contract_cols(query, k_ref[0:TRUNK, :]) * scale
        pieces.append(jnp.where(causal(TRUNK), score, NEGATIVE))
    else:
        if TRUNK * chunk < LEAF_END:
            pieces.append(contract_cols(query, k_ref[0:TRUNK, :]) * scale)
        mask = jnp.concatenate([causal(SEG)] * 4, 0)
        pieces.append(jnp.where(mask, seg_dot(query, k_ref, blocks[0]) * scale, NEGATIVE))
        for starts in blocks[1:]:
            pieces.append(seg_dot(query, k_ref, starts) * scale)
    highest = jnp.max(pieces[0], -1, keepdims=True)
    for piece in pieces[1:]:
        highest = jnp.maximum(highest, jnp.max(piece, -1, keepdims=True))
    raised = [jnp.exp(piece - highest) for piece in pieces]
    total = jnp.sum(raised[0], -1, keepdims=True)
    for piece in raised[1:]:
        total = total + jnp.sum(piece, -1, keepdims=True)
    inverse = 1.0 / total
    return [piece * inverse for piece in raised]


def chunk_parts(chunk, pieces, blocks):
    places = []
    if chunk == 0:
        places = [None]
    else:
        if TRUNK * chunk < LEAF_END:
            places.append(None)
        places = places + blocks
    return list(zip(pieces, places))


def forward_kernel(
    parents_ref,
    q_ref,
    k_ref,
    v_ref,
    qs_ref,
    ks_ref,
    qg_ref,
    kg_ref,
    cos_ref,
    sin_ref,
    att_ref,
    qr_ref,
    kr_ref,
    vl_ref,
):
    tree = pl.program_id(0)
    scale = 1.0 / math.sqrt(HD)
    parent_of = [parents_ref[tree, s] for s in range(NSEG)]

    def turned(field):
        return field * cos_ref[...] + pltpu.roll(field, HD // 2, 1) * sin_ref[...]

    qr_ref[...] = turned(q_ref[...] * qs_ref[...] * qg_ref[...]).astype(jnp.bfloat16)
    kr_ref[...] = turned(k_ref[...] * ks_ref[...] * kg_ref[...]).astype(jnp.bfloat16)
    vl_ref[...] = v_ref[...].astype(jnp.bfloat16)
    for chunk in range(TREE // TRUNK):
        rows = slice(chunk * TRUNK, (chunk + 1) * TRUNK)
        blocks = key_starts(chunk, parent_of)
        weights = chunk_weights(chunk, qr_ref[rows, :], kr_ref, blocks, scale)
        total = jnp.zeros((TRUNK, HD), jnp.float32)
        for weight, starts in chunk_parts(chunk, weights, blocks):
            low = weight.astype(jnp.bfloat16)
            if starts is None:
                total = total + dot_f32(low, vl_ref[0:TRUNK, :], 1, 0)
            else:
                total = total + jnp.concatenate(
                    [
                        dot_f32(
                            low[s * SEG : (s + 1) * SEG], vl_ref[pl.ds(starts[s], SEG), :], 1, 0
                        )
                        for s in range(4)
                    ],
                    0,
                )
        att_ref[rows, :] = total.astype(jnp.bfloat16)


def backward_kernel(
    parents_ref,
    qr_ref,
    kr_ref,
    vl_ref,
    do_ref,
    cos_ref,
    sin_ref,
    dq_ref,
    dk_ref,
    dv_ref,
    dv_acc,
):
    tree = pl.program_id(0)
    scale = 1.0 / math.sqrt(HD)
    parent_of = [parents_ref[tree, s] for s in range(NSEG)]
    dk_ref[...] = jnp.zeros_like(dk_ref)
    dv_acc[...] = jnp.zeros_like(dv_acc)
    for chunk in range(TREE // TRUNK):
        rows = slice(chunk * TRUNK, (chunk + 1) * TRUNK)
        blocks = key_starts(chunk, parent_of)
        query = qr_ref[rows, :]
        grad = do_ref[rows, :]
        weights = chunk_weights(chunk, query, kr_ref, blocks, scale)
        parts = chunk_parts(chunk, weights, blocks)
        d_weights = []
        row_dot = jnp.zeros((TRUNK, 1), jnp.float32)
        for weight, starts in parts:
            if starts is None:
                d_weight = contract_cols(grad, vl_ref[0:TRUNK, :])
            else:
                d_weight = seg_dot(grad, vl_ref, starts)
            d_weights.append(d_weight)
            row_dot = row_dot + jnp.sum(weight * d_weight, -1, keepdims=True)
        d_query = jnp.zeros((TRUNK, HD), jnp.float32)
        for (weight, starts), d_weight in zip(parts, d_weights):
            low = weight.astype(jnp.bfloat16)
            d_score = (weight * (d_weight - row_dot)).astype(jnp.bfloat16)
            if starts is None:
                d_query = d_query + dot_f32(d_score, kr_ref[0:TRUNK, :], 1, 0)
                dk_ref[0:TRUNK, :] += contract_rows(d_score, query)
                dv_acc[0:TRUNK, :] += contract_rows(low, grad)
            else:
                turns = []
                for s in range(4):
                    own = slice(s * SEG, (s + 1) * SEG)
                    keys = pl.ds(starts[s], SEG)
                    turns.append(dot_f32(d_score[own], kr_ref[keys, :], 1, 0))
                    dk_ref[keys, :] += contract_rows(d_score[own], query[own])
                    dv_acc[keys, :] += contract_rows(low[own], grad[own])
                d_query = d_query + jnp.concatenate(turns, 0)
        dq_ref[rows, :] = d_query

    def unturned(field):
        return (field * cos_ref[...] - pltpu.roll(field, HD // 2, 1) * sin_ref[...]) * scale

    dq_ref[...] = unturned(dq_ref[...])
    dk_ref[...] = unturned(dk_ref[...])
    dv_ref[...] = dv_acc[...].astype(jnp.bfloat16)


def attend(parents, qkv, q_scale, k_scale, q_gain, k_gain, cos_table, sin_table, heads):
    trees = parents.shape[0]
    rows = qkv.shape[0]

    def field(shift):
        return pl.BlockSpec((TREE, HD), lambda t, h, p: (t, h + shift))

    scale_spec = pl.BlockSpec((TREE, 1), lambda t, h, p: (t, 0))
    gain_spec = pl.BlockSpec((1, HD), lambda t, h, p: (0, h))
    table = pl.BlockSpec((TREE, HD), lambda t, h, p: (t, 0))
    return pl.pallas_call(
        forward_kernel,
        grid_spec=pltpu.PrefetchScalarGridSpec(
            num_scalar_prefetch=1,
            grid=(trees, heads),
            in_specs=[
                field(0),
                field(heads),
                field(2 * heads),
                scale_spec,
                scale_spec,
                gain_spec,
                gain_spec,
                table,
                table,
            ],
            out_specs=[field(0)] * 4,
        ),
        out_shape=[jax.ShapeDtypeStruct((rows, heads * HD), jnp.bfloat16)] * 4,
        compiler_params=pltpu.CompilerParams(vmem_limit_bytes=50 * MIB),
        name="tree_forward",
    )(
        parents,
        qkv,
        qkv,
        qkv,
        q_scale,
        k_scale,
        q_gain[None, :],
        k_gain[None, :],
        cos_table,
        sin_table,
    )


def attend_back(parents, q_rot, k_rot, values, d_attended, cos_table, sin_table, heads):
    trees = parents.shape[0]
    rows = q_rot.shape[0]
    field = pl.BlockSpec((TREE, HD), lambda t, h, p: (t, h))
    table = pl.BlockSpec((TREE, HD), lambda t, h, p: (t, 0))
    return pl.pallas_call(
        backward_kernel,
        grid_spec=pltpu.PrefetchScalarGridSpec(
            num_scalar_prefetch=1,
            grid=(trees, heads),
            in_specs=[field, field, field, field, table, table],
            out_specs=[field] * 3,
            scratch_shapes=[pltpu.VMEM((TREE, HD), jnp.float32)],
        ),
        out_shape=[
            jax.ShapeDtypeStruct((rows, heads * HD), jnp.float32),
            jax.ShapeDtypeStruct((rows, heads * HD), jnp.float32),
            jax.ShapeDtypeStruct((rows, heads * HD), jnp.bfloat16),
        ],
        compiler_params=pltpu.CompilerParams(vmem_limit_bytes=50 * MIB),
        name="tree_backward",
    )(parents, q_rot, k_rot, values, d_attended, cos_table, sin_table)


def slots_kernel(slot_ref, gate_ref, gain_ref, x_ref, *refs, normed):
    units = slot_ref.shape[1]
    outs, gate_out, acc, gate_acc = refs[:units], refs[units], refs[units + 1], refs[units + 2]
    step = pl.program_id(1)

    @pl.when(step == 0)
    def _():
        acc[...] = jnp.zeros_like(acc)
        gate_acc[...] = jnp.zeros_like(gate_acc)

    for e in range(units):
        slots = lax.broadcasted_iota(jnp.int32, (CAPP, x_ref.shape[0]), 0)
        picks = slot_ref[0, e : e + 1, :] == slots
        acc[e] += dot_f32(picks.astype(jnp.bfloat16), x_ref[...], 1, 0)
        gate_acc[e] += jnp.sum(jnp.where(picks, gate_ref[0, e : e + 1, :], 0.0), 1, keepdims=True)

    @pl.when(step == pl.num_programs(1) - 1)
    def _():
        for e in range(units):
            rows = acc[e]
            if normed:
                scale = lax.rsqrt(jnp.mean(rows * rows, 1, keepdims=True) + EPS)
                outs[e][...] = (rows * scale * gain_ref[...]).astype(jnp.bfloat16)
            else:
                outs[e][...] = (gate_acc[e] * rows).astype(jnp.bfloat16)
            gate_out[e] = gate_acc[e]


def to_slots(slot_of, token_gate, gain, rows, normed):
    groups, units, tok_rows = slot_of.shape
    width = rows.shape[1]
    block = tok_rows // 2
    steps = tok_rows // block
    table = pl.BlockSpec((1, units, block), lambda g, t: (g, 0, t))
    out = pl.pallas_call(
        functools.partial(slots_kernel, normed=normed),
        grid=(groups, steps),
        in_specs=[
            table,
            table,
            pl.BlockSpec((1, width), lambda g, t: (0, 0)),
            pl.BlockSpec((block, width), lambda g, t: (g * steps + t, 0)),
        ],
        out_specs=[pl.BlockSpec((CAPP, width), lambda g, t: (g, 0))] * units
        + [pl.BlockSpec((units, CAPP, 1), lambda g, t: (0, g, 0))],
        out_shape=[jax.ShapeDtypeStruct((groups * CAPP, width), jnp.bfloat16)] * units
        + [jax.ShapeDtypeStruct((units, groups * CAPP, 1), jnp.float32)],
        scratch_shapes=[
            pltpu.VMEM((units, CAPP, width), jnp.float32),
            pltpu.VMEM((units, CAPP, 1), jnp.float32),
        ],
        compiler_params=pltpu.CompilerParams(vmem_limit_bytes=56 * MIB),
        cost_estimate=pl.CostEstimate(
            flops=2 * groups * tok_rows * units * CAPP * width,
            bytes_accessed=2 * groups * tok_rows * width,
            transcendentals=0,
        ),
        name="slots",
    )(slot_of, token_gate, gain[None, :], rows)
    return out[:units], out[units]


def combine_kernel(slot_ref, *refs):
    out_ref = refs[-1]
    total = None
    for e, y_ref in enumerate(refs[:-1]):
        slots = lax.broadcasted_iota(jnp.int32, (slot_ref.shape[0], CAPP), 1)
        picks = (slot_ref[:, e : e + 1] == slots).astype(jnp.bfloat16)
        term = dot_f32(picks, y_ref[0], 1, 0)
        total = term if total is None else total + term
    out_ref[...] = total.astype(out_ref.dtype)


def combine(slot_of, slot_rows, tok_rows, half=None):
    units, width = len(slot_rows), slot_rows[0].shape[1]
    groups = slot_rows[0].shape[0] // CAPP
    block = tok_rows // 4
    steps = 4 if half is None else 2
    first = 0 if half is None else 2 * half
    rows_spec = pl.BlockSpec((1, CAPP, width), lambda g, t: (g, 0, 0))
    return pl.pallas_call(
        combine_kernel,
        grid=(groups, steps),
        in_specs=[pl.BlockSpec((block, units), lambda g, t: (g * 4 + first + t, 0))]
        + [rows_spec] * units,
        out_specs=pl.BlockSpec((block, width), lambda g, t: (g * steps + t, 0)),
        out_shape=jax.ShapeDtypeStruct((groups * steps * block, width), jnp.bfloat16),
        compiler_params=pltpu.CompilerParams(vmem_limit_bytes=50 * MIB),
        cost_estimate=pl.CostEstimate(
            flops=2 * groups * steps * block * units * CAPP * width,
            bytes_accessed=2 * groups * steps * block * width,
            transcendentals=0,
        ),
        name="combine",
    )(slot_of, *[rows.reshape(groups, CAPP, width) for rows in slot_rows])


def shift_row(block, k):
    count = lax.axis_size("row")
    return lax.ppermute(block, "row", [(i, (i + k) % count) for i in range(count)])


def row_stack(part, *earlier):
    count = lax.axis_size("row")
    here = lax.axis_index("row")
    part = after(part, *earlier)
    whole = jnp.zeros((count,) + part.shape, part.dtype)
    for k in range(count):
        block = part if k == 0 else shift_row(part, k)
        whole = lax.dynamic_update_slice_in_dim(whole, block[None], (here - k) % count, 0)
    return whole


def crossing_units():
    count = lax.axis_size("row")
    units = []
    for k in range(1, count):
        parts = 1 if k in (1, count - 1) else 2
        units = units + [(k, part, parts) for part in range(parts)]
    return units


def home_unit(weight, unit, *earlier):
    k, part, parts = unit
    groups = lax.axis_size("row")
    share = weight.shape[1] // groups
    to = (lax.axis_index("row") + k) % groups
    block = lax.dynamic_slice_in_dim(
        after(weight, *earlier), to * share + part * (share // parts), share // parts, 1
    )
    return shift_row(block, k)


def home_kernel(here_ref, own_ref, *refs, units, groups):
    out_ref = refs[-1]
    source = lax.rem(here_ref[0] - pl.program_id(0) + groups, groups)

    @pl.when(source == 0)
    def _():
        out_ref[...] = own_ref[...]

    for (k, part, parts), block_ref in zip(units, refs[:-1]):
        wide = out_ref.shape[1] // parts

        @pl.when(source == k)
        def _(block_ref=block_ref, start=part * wide, wide=wide):
            out_ref[:, start : start + wide] = block_ref[...]


def at_home(weight, units, blocks):
    groups = lax.axis_size("row")
    depth, columns = weight.shape
    share = columns // groups
    return pl.pallas_call(
        functools.partial(home_kernel, units=units, groups=groups),
        grid_spec=pltpu.PrefetchScalarGridSpec(
            num_scalar_prefetch=1,
            grid=(groups,),
            in_specs=[pl.BlockSpec((depth, share), lambda j, here: (0, here[0]))]
            + [pl.BlockSpec(block.shape, lambda j, here: (0, 0)) for block in blocks],
            out_specs=pl.BlockSpec((depth, share), lambda j, here: (j, 0)),
        ),
        out_shape=jax.ShapeDtypeStruct((depth * groups, share), weight.dtype),
        compiler_params=pltpu.CompilerParams(vmem_limit_bytes=50 * MIB),
        cost_estimate=pl.CostEstimate(
            flops=0, bytes_accessed=4 * depth * columns, transcendentals=0
        ),
        name="at_home",
    )(lax.axis_index("row").astype(jnp.int32)[None], weight, *blocks)


def back_units(count):
    rows = lax.axis_size("row")
    units = []
    for k in range(1, rows):
        if k in (1, rows - 1):
            units.append((k, tuple(range(count))))
        else:
            units = units + [(k, (e,)) for e in range(count)]
    return units


def back_unit(grads, unit, *earlier):
    k, which = unit
    groups = lax.axis_size("row")
    depth = grads[0].shape[0] // groups
    to = (lax.axis_index("row") + k) % groups
    chosen = after([grads[e] for e in which], *earlier)
    return [
        shift_row(lax.dynamic_slice_in_dim(grad, to * depth, depth, 0), k) for grad in chosen
    ]


def owner_kernel(here_ref, *refs, units, groups, count):
    out_ref = refs[-1]
    hidden = refs[0].shape[1]
    source = lax.rem(here_ref[0] - pl.program_id(0) + groups, groups)
    places = [(0, e) for e in range(count)]
    places = places + [(k, e) for k, which in units for e in which]
    for (k, e), block_ref in zip(places, refs[:-1]):

        @pl.when(source == k)
        def _(block_ref=block_ref, start=e * hidden):
            out_ref[:, start : start + hidden] = block_ref[...].astype(jnp.float32)


def at_owner(grads, units, received):
    groups = lax.axis_size("row")
    depth, hidden = grads[0].shape[0] // groups, grads[0].shape[1]
    count = len(grads)
    share = hidden * count
    blocks = [block for pair in received for block in pair]
    return pl.pallas_call(
        functools.partial(owner_kernel, units=units, groups=groups, count=count),
        grid_spec=pltpu.PrefetchScalarGridSpec(
            num_scalar_prefetch=1,
            grid=(groups,),
            in_specs=[pl.BlockSpec((depth, hidden), lambda j, here: (here[0], 0))] * count
            + [pl.BlockSpec((depth, hidden), lambda j, here: (0, 0))] * len(blocks),
            out_specs=pl.BlockSpec((depth, share), lambda j, here: (0, j)),
        ),
        out_shape=jax.ShapeDtypeStruct((depth, share * groups), jnp.float32),
        compiler_params=pltpu.CompilerParams(vmem_limit_bytes=50 * MIB),
        cost_estimate=pl.CostEstimate(
            flops=0, bytes_accessed=6 * depth * share * groups, transcendentals=0
        ),
        name="at_owner",
    )(lax.axis_index("row").astype(jnp.int32)[None], *grads, *blocks)


def line_steps(part, *earlier):
    count = lax.axis_size("row")
    upward = downward = part
    steps = []
    for _ in range(count - 1):
        upward, downward = after((upward, downward), *earlier)
        upward = lax.ppermute(upward, "row", [(i, i + 1) for i in range(count - 1)])
        downward = lax.ppermute(downward, "row", [(i + 1, i) for i in range(count - 1)])
        earlier = (upward, downward)
        steps.append((upward, downward))
    return steps


def line_gather(part, steps):
    count = lax.axis_size("row")
    here = lax.axis_index("row")
    rows = part.shape[0]
    whole = jnp.zeros((rows * count, part.shape[1]), part.dtype)
    whole = lax.dynamic_update_slice_in_dim(whole, part, here * rows, 0)
    for k in range(1, count):
        block = jnp.where(here >= k, steps[k - 1][0], steps[count - k - 1][1])
        whole = lax.dynamic_update_slice_in_dim(whole, block, ((here - k) % count) * rows, 0)
    return whole


def group_total(part, along=(), beside=None):
    groups = lax.axis_size("row")
    here = lax.axis_index("row")
    rows = part.shape[0] // groups

    def rows_of(group):
        start = jnp.clip(group, 0, groups - 1) * rows
        return lax.dynamic_slice_in_dim(part, start, rows, 0).astype(jnp.float32)

    upward = downward = 0.0
    for step in range(1, groups):
        upward = (rows_of(here + groups - step) + upward).astype(jnp.bfloat16)
        downward = (rows_of(here - groups + step) + downward).astype(jnp.bfloat16)
        upward = lax.ppermute(upward, "row", [(i, i + 1) for i in range(step)])
        downward = lax.ppermute(downward, "row", [(groups - 1 - i, groups - 2 - i) for i in range(step)])
        ties = along if step == groups - 2 else ()
        if step == groups - 1 and beside is not None:
            ties = beside()
        upward, downward = after((upward, downward), *ties)
        upward, downward = upward.astype(jnp.float32), downward.astype(jnp.float32)
    return rows_of(here) + upward + downward


def body(
    tokens,
    attn_norm,
    w_query,
    w_key,
    w_value,
    q_norm,
    k_norm,
    w_out,
    moe_norm,
    w_gate,
    w_up,
    w_down,
    routes,
    gates,
    parents,
    cotangent,
):
    tok_rows, own_width = tokens.shape
    groups = lax.axis_size("row")
    cols = lax.axis_size("col")
    width = own_width * cols
    here, col = lax.axis_index("row"), lax.axis_index("col")
    col_start = col * own_width
    heads = own_width // HD
    trees = parents.shape[0]

    qkv_cols = lax.all_gather(
        jnp.concatenate([w_query, w_key, w_value], 1), "row", axis=0, tiled=True
    )
    out_cols = lax.all_gather(after(w_out, qkv_cols), "row", axis=0, tiled=True)
    shifts = crossing_units()
    last = len(shifts) - 1
    grad_steps = line_steps(cotangent, qkv_cols)

    wide = jnp.concatenate(gather_blocks(tokens), 1).astype(jnp.float32)
    cos_table, sin_table = jax.vmap(rope_tables)(parents)
    cos_table, sin_table = cos_table.reshape(-1, HD), sin_table.reshape(-1, HD)
    scale_one = lax.rsqrt(jnp.mean(wide * wide, 1, keepdims=True) + EPS)
    norm_gain = block_order(attn_norm, own_width)
    normed_one = (wide * scale_one * norm_gain[None, :]).astype(jnp.bfloat16)
    qkv_cols = block_order(qkv_cols, own_width)
    qkv = jnp.dot(normed_one, qkv_cols, preferred_element_type=jnp.float32)
    query, keyed = qkv[:, :own_width], qkv[:, own_width : 2 * own_width]
    squares = over_col(jnp.stack([jnp.sum(query * query, 1), jnp.sum(keyed * keyed, 1)]))
    q_scale = lax.rsqrt(squares[0] / width + EPS)[:, None]
    k_scale = lax.rsqrt(squares[1] / width + EPS)[:, None]
    q_gain = lax.dynamic_slice_in_dim(q_norm, col_start, own_width)
    k_gain = lax.dynamic_slice_in_dim(k_norm, col_start, own_width)
    attended, q_rot, k_rot, value_low = attend(
        parents, qkv, q_scale, k_scale, q_gain, k_gain, cos_table, sin_table, heads
    )
    attn_sum = lax.psum_scatter(
        after(contract_cols(attended, out_cols).astype(jnp.bfloat16), grad_steps[0]),
        "col",
        scatter_dimension=1,
        tiled=True,
    )
    route_all = row_stack(routes.T, grad_steps[0])
    gate_all = row_stack(gates.T, grad_steps[0])
    gate_units = [home_unit(w_gate, shifts[0], grad_steps[:-1])]
    attn_sum = after(attn_sum, gate_units, grad_steps, route_all, gate_all)
    residual = tokens.astype(jnp.float32) + attn_sum.astype(jnp.float32)
    mid_low = residual.astype(jnp.bfloat16)
    mid_own = mid_low.astype(jnp.float32)
    mid_row = lax.all_gather(mid_low, "row", axis=0, tiled=True)
    gate_units.append(home_unit(w_gate, shifts[1], mid_low))
    grad_row = line_gather(cotangent, grad_steps)

    share = w_gate.shape[1] // groups
    units, hidden_units = max(1, share // FF), min(share, FF)
    first_unit = col * (w_gate.shape[1] // FF) + (here * share) // FF
    unit_ids = first_unit + jnp.arange(units, dtype=jnp.int32)
    match = route_all[None] == unit_ids[:, None, None, None]
    named = jnp.any(match, 2)
    token_gate = jnp.sum(jnp.where(match, gate_all[None], 0.0), 2)
    rank = jnp.cumsum(named.astype(jnp.int32), 2) - 1
    slot_of = jnp.where(named, rank, -1)
    slot_of, token_gate = slot_of.transpose(1, 0, 2), token_gate.transpose(1, 0, 2)
    slot_column = slot_of.transpose(0, 2, 1).reshape(groups * tok_rows, units)
    mid_row, slot_of, token_gate, slot_column, grad_row = after(
        (mid_row, slot_of, token_gate, slot_column, grad_row), gate_units
    )
    mid_all = lax.all_gather(mid_row, "col", axis=1, tiled=True)
    scale_two = lax.rsqrt(over_col(jnp.sum(mid_own * mid_own, 1)) / width + EPS)[:, None]
    for unit in shifts[2:]:
        gate_units.append(home_unit(w_gate, unit, gate_units[-1], mid_row))
    gate_home = at_home(w_gate, shifts, gate_units)
    up_units = [home_unit(w_up, shifts[0], gate_units[-1])]
    for unit in shifts[1:last]:
        up_units.append(home_unit(w_up, unit, up_units[-1]))
    mid_all, gate_home = after((mid_all, gate_home), up_units[-2])
    grad_all = lax.all_gather(after(grad_row, mid_all), "col", axis=1, tiled=True)

    experts = range(units)
    cut = [slice(e * hidden_units, (e + 1) * hidden_units) for e in experts]
    expert_in, slot_gate = to_slots(slot_of, token_gate, moe_norm, mid_all, True)
    expert_in = after(expert_in, up_units[-1])
    up_units = after(up_units, expert_in)
    up_units.append(home_unit(w_up, shifts[last], up_units[-1], expert_in))
    gate_acts = [dot_f32(expert_in[e], gate_home[:, cut[e]], 1, 0) for e in experts]
    up_home, gate_acts = after((at_home(w_up, shifts, up_units), gate_acts))
    down_units = [home_unit(w_down, shifts[0], up_home)]
    acts = []
    for e in experts:
        up_act = dot_f32(expert_in[e], up_home[:, cut[e]], 1, 0)
        sigmoid_gate = jax.nn.sigmoid(gate_acts[e])
        silu_gate = gate_acts[e] * sigmoid_gate
        hidden = (silu_gate * up_act).astype(jnp.bfloat16)
        acts.append((gate_acts[e], up_act, sigmoid_gate, silu_gate, hidden))
    hiddens = after([act[-1] for act in acts], down_units[0])
    down_units.append(home_unit(w_down, shifts[1], hiddens))
    grad_all = after(grad_all, down_units[1])
    for unit in shifts[2:last]:
        down_units.append(home_unit(w_down, unit, grad_all))
    d_out, _ = to_slots(slot_of, token_gate, moe_norm, grad_all, False)
    d_out = after(d_out, down_units[-1])
    down_units.append(home_unit(w_down, shifts[last], d_out))
    leaving = back_units(units)
    early, late = leaving[1:2], [leaving[0]] + leaving[2:]
    down_grads = [contract_rows(d_out[0], hiddens[0]).astype(jnp.bfloat16)]
    down_grads, d_out, hiddens, down_units = after((down_grads, d_out, hiddens, down_units))
    down_back = [back_unit(down_grads, unit) for unit in early]
    for e in experts[1:]:
        down_grads.append(contract_rows(d_out[e], hiddens[e]).astype(jnp.bfloat16))
    down_home = at_home(w_down, shifts, down_units)
    down_grads, down_home, d_out = after((down_grads, down_home, d_out))

    d_acts, terms = [], []
    for e in experts:
        gate_act, up_act, sigmoid_gate, silu_gate, _ = acts[e]
        d_hidden = dot_f32(d_out[e], down_home[:, cut[e]], 1, 0)
        d_gate = (
            d_hidden * up_act * sigmoid_gate * (1.0 + gate_act * (1.0 - sigmoid_gate))
        ).astype(jnp.bfloat16)
        d_acts.append((d_gate, (d_hidden * silu_gate).astype(jnp.bfloat16)))
        terms.append(contract_cols(d_gate, gate_home[:, cut[e]]))
        if e == 0:
            terms, d_acts, d_out = after((terms, d_acts, d_out), down_back)
            down_back.append(back_unit(down_grads, late[0], terms))
    terms, d_acts = after((terms, d_acts), down_back)
    for unit in late[1:-1]:
        down_back.append(back_unit(down_grads, unit, terms))
    d_in = [
        (terms[e] + contract_cols(d_acts[e][1], up_home[:, cut[e]])).astype(jnp.bfloat16)
        for e in experts
    ]
    d_rows = combine(slot_column, d_in, tok_rows)
    d_rows, expert_in, d_acts = after((d_rows, expert_in, d_acts), down_back)
    down_back.append(back_unit(down_grads, late[-1], d_rows))
    d_rows = lax.psum_scatter(d_rows, "col", scatter_dimension=1, tiled=True)
    gate_grads = [contract_rows(expert_in[e], d_acts[e][0]).astype(jnp.bfloat16) for e in experts]
    up_grads = [contract_rows(expert_in[e], d_acts[e][1]).astype(jnp.bfloat16) for e in experts]
    gate_grads, up_grads, hiddens = after((gate_grads, up_grads, hiddens), down_back[-1])
    gate_back = [back_unit(gate_grads, leaving[0])]
    gate_back.append(back_unit(gate_grads, leaving[1]))
    gated = [
        (slot_gate[e] * contract_cols(hiddens[e], down_home[:, cut[e]])).astype(jnp.bfloat16)
        for e in experts
    ]
    halves = [combine(slot_column, gated, tok_rows, half) for half in (0, 1)]
    halves = after(halves, gate_back)
    for unit in leaving[2:]:
        gate_back.append(back_unit(gate_grads, unit, halves))
    d_rows = after(d_rows, gate_back)
    up_back = [back_unit(up_grads, leaving[0], d_rows)]
    d_normed_two = group_total(d_rows, up_back[0])
    halves[0] = lax.psum_scatter(
        after(halves[0], d_rows), "col", scatter_dimension=1, tiled=True
    )
    w_down_grad = at_owner(down_grads, early + late, down_back)
    w_gate_grad = at_owner(gate_grads, leaving, gate_back)

    gain_two = lax.dynamic_slice_in_dim(moe_norm, col_start, own_width)
    moe_dot = over_col(jnp.sum(d_normed_two * gain_two * mid_own, 1))
    d_residual = (
        cotangent.astype(jnp.float32)
        + scale_two * gain_two * d_normed_two
        - mid_own * scale_two**3 * (moe_dot / width)[:, None]
    )
    moe_gain_grad = jnp.sum(d_normed_two * mid_own * scale_two, 0)
    d_res_low = d_residual.astype(jnp.bfloat16)
    up_back.append(back_unit(up_grads, leaving[1], d_normed_two))
    d_res_low, halves[0], w_down_grad = after((d_res_low, halves[0], w_down_grad))
    d_attn_whole = lax.all_gather(d_res_low, "col", axis=1, tiled=True)
    d_attn_whole, w_gate_grad = after((d_attn_whole, w_gate_grad), up_back)
    halves[1] = lax.psum_scatter(
        after(halves[1], d_attn_whole), "col", scatter_dimension=1, tiled=True
    )
    moe_sums = [group_total(after(halves[0], d_attn_whole))]
    d_attended = jnp.dot(
        d_attn_whole, out_cols, preferred_element_type=jnp.float32
    ).astype(jnp.bfloat16)
    d_qn, d_kn, d_values = attend_back(
        parents, q_rot, k_rot, value_low, d_attended, cos_table, sin_table, heads
    )
    qk_dots = over_col(
        jnp.stack([jnp.sum(query * q_gain * d_qn, 1), jnp.sum(keyed * k_gain * d_kn, 1)])
    )
    up_back.append(back_unit(up_grads, leaving[2], d_attn_whole))
    qk_dots = after(qk_dots, moe_sums[0], up_back)
    for unit in leaving[3:]:
        up_back.append(back_unit(up_grads, unit, up_back[2], qk_dots))
    d_query = (
        q_scale * q_gain * d_qn - query * q_scale**3 * (qk_dots[0] / width)[:, None]
    ).astype(jnp.bfloat16)
    d_keyed = (
        k_scale * k_gain * d_kn - keyed * k_scale**3 * (qk_dots[1] / width)[:, None]
    ).astype(jnp.bfloat16)
    q_gain_grad = jnp.sum(d_qn * query * q_scale, 0)
    k_gain_grad = jnp.sum(d_kn * keyed * k_scale, 0)
    d_qkv = jnp.concatenate([d_query, d_keyed, d_values], 1)
    d_one = block_order(contract_cols(qkv_cols, d_qkv).astype(jnp.bfloat16), own_width)
    d_qkv, attended, d_attn_whole = after((d_qkv, attended, d_attn_whole), d_one)
    attn_grads = jnp.concatenate(
        [
            block_order(contract_rows(normed_one, d_qkv).astype(jnp.bfloat16), own_width),
            contract_rows(d_attn_whole, attended).astype(jnp.bfloat16),
        ],
        1,
    )
    d_one, attn_grads, halves[1] = after((d_one, attn_grads, halves[1]), up_back[-1])
    w_up_grad = at_owner(up_grads, leaving, up_back)
    d_normed_one = lax.psum_scatter(d_one, "col", scatter_dimension=0, tiled=True)
    attn_grads = group_total(attn_grads)
    d_normed_one = d_normed_one.astype(jnp.float32).T
    w_query_grad = attn_grads[:, :own_width]
    w_key_grad = attn_grads[:, own_width : 2 * own_width]
    w_value_grad = attn_grads[:, 2 * own_width : 3 * own_width]
    w_out_grad = attn_grads[:, 3 * own_width :]
    tokens_own = tokens.astype(jnp.float32)
    gain_one = lax.dynamic_slice_in_dim(attn_norm, col_start, own_width)
    attn_dot = over_col(jnp.sum(d_normed_one * gain_one * tokens_own, 1))
    tokens_grad = (
        d_residual
        + scale_one * gain_one * d_normed_one
        - tokens_own * scale_one**3 * (attn_dot / width)[:, None]
    )
    attn_gain_grad = jnp.sum(d_normed_one * tokens_own * scale_one, 0)
    gain_grads = jnp.sum(
        row_stack(jnp.stack([attn_gain_grad, q_gain_grad, k_gain_grad, moe_gain_grad])), 0
    )
    moe_sums.append(group_total(halves[1], beside=lambda: (gain_grads, tokens_grad, w_up_grad)))
    moe_sum = jnp.concatenate(moe_sums, 0)
    output = (residual + moe_sum).astype(jnp.bfloat16)
    return (
        output,
        tokens_grad,
        gain_grads[0],
        w_query_grad,
        w_key_grad,
        w_value_grad,
        gain_grads[1],
        gain_grads[2],
        w_out_grad,
        gain_grads[3],
        w_gate_grad,
        w_up_grad,
        w_down_grad,
    )


def solution(mesh):
    grid = P("row", "col")
    rows = P("row", None)
    in_specs = (
        grid,
        P(),
        grid,
        grid,
        grid,
        P(),
        P(),
        grid,
        P(),
        grid,
        grid,
        grid,
        rows,
        rows,
        rows,
        grid,
    )
    out_specs = (
        grid,
        grid,
        P("col"),
        grid,
        grid,
        grid,
        P("col"),
        P("col"),
        grid,
        P("col"),
        grid,
        grid,
        grid,
    )
    return jax.shard_map(body, mesh=mesh, in_specs=in_specs, out_specs=out_specs, check_vma=False)
```
